32 devices in a mesh: groups: 2 (over y), dp: 8 (over z, x), seq: 2 (over core).
Axes of the slice: x: 2, y: 2, z: 4, core: 2. Of those that a mesh axis runs over, the one named last changes fastest.
Arguments:
- query_rows: bfloat16 [6144, 1280], P(('groups', 'dp', 'seq')), parts along dimension 0, may hold values from -8 to 8
- key_rows: bfloat16 [6144, 1280], P(('groups', 'dp', 'seq')), parts along dimension 0, may hold values from -8 to 8
- value_rows: bfloat16 [6144, 1280], P(('groups', 'dp', 'seq')), parts along dimension 0, may hold values from -6 to 6
- grad_hosted: bfloat16 [8192, 1280], P(('groups', 'dp', 'seq')), parts along dimension 0, may hold values from -6 to 6
- image_grid: int32 [16, 2, 2], P('groups'), parts along dimension 0, may hold values from 8 to 16, as said below
- destination: int32 [16, 2], P('groups'), parts along dimension 0, may hold values from 0 to 7, as said below
Outputs:
- hosted_out: bfloat16 [8192, 1280], P(('groups', 'dp', 'seq')), parts along dimension 0
- grad_query: bfloat16 [6144, 1280], P(('groups', 'dp', 'seq')), parts along dimension 0
- grad_key: bfloat16 [6144, 1280], P(('groups', 'dp', 'seq')), parts along dimension 0
- grad_value: bfloat16 [6144, 1280], P(('groups', 'dp', 'seq')), parts along dimension 0
The draws below stay inside these ranges and needn't reach their ends.
There are 2 independent parts, one for each index of `groups`. The reference program is written for one: setup_inputs(seed, part) draws one part's arguments, and reference() takes and returns one part's arrays. A program takes and returns all parts, laid end to end along the dimension named above; each array names one. Nothing has to cross between parts.
Inputs may be any that keep to these rules, and one draw needn't show every extreme that they name: `image_grid`: a rank's images together hold at most 384 patches; some rank lists an image of 16 x 16 patches and exactly 384 patches in all. `destination`: each column is a permutation of the ranks: every rank hosts exactly one image of each list position.
All inputs are finite; a program needn't handle non-finite values.
Results may differ from the reference program's by a relative error of at most 0.012.
The reference program's roundings to bfloat16 on the way (of `probs_bf` and `grad_scores`) count: a program that leaves them out, or rounds other values in their place, can miss the bound.
Values may be sent and summed in bfloat16 or wider, within the bound.
No kernel may reach another device: no remote copies, remote signals or barrier semaphores. Data moves between devices by JAX's collectives and lax.ppermute only.
A program may use at most 64 MiB of HBM per device.

```python
import jax
import jax.numpy as jnp
from jax import lax

D = 1280
HEADS = 16
HEAD_DIM = 80
SIDE = 16
IMGS = 2
MAXLEN = 256
RANK_ROWS = 384
TOKENS = 3072
HOSTED = 4096
N_DP = 8


def draw_query_rows(key, part):
    key = jax.random.fold_in(key, 21)
    result = jax.random.normal(key, (TOKENS, D), jnp.float32)
    return jnp.clip(result, -8.0, 8.0).astype(jnp.bfloat16)


def draw_key_rows(key, part):
    key = jax.random.fold_in(key, 22)
    result = jax.random.normal(key, (TOKENS, D), jnp.float32)
    return jnp.clip(result, -8.0, 8.0).astype(jnp.bfloat16)


def draw_image_grid(key, part):
    key = jax.random.fold_in(key, 11)
    lowest = SIDE // 2
    heights = jax.random.randint(jax.random.fold_in(key, 1), (N_DP, IMGS), lowest, SIDE + 1)
    widths = jax.random.randint(jax.random.fold_in(key, 2), (N_DP, IMGS), lowest, SIDE + 1)
    full_rank = jax.random.randint(jax.random.fold_in(key, 3), (), 0, N_DP)
    is_full = jnp.arange(N_DP, dtype=jnp.int32)[:, None] == full_rank
    heights = jnp.where(is_full, SIDE, heights)
    widths = jnp.where(is_full, SIDE, widths)
    used = heights[:, 0] * widths[:, 0]
    columns = [heights[:, 0]]
    for index in range(1, IMGS):
        room = RANK_ROWS - used
        capped = jnp.minimum(heights[:, index], room // widths[:, index])
        columns.append(capped)
        used = used + capped * widths[:, index]
    heights = jnp.stack(columns, axis=1)
    return jnp.stack([heights, widths], axis=-1).astype(jnp.int32)


def draw_destination(key, part):
    key = jax.random.fold_in(key, 12)
    columns = [jax.random.permutation(jax.random.fold_in(key, index), N_DP) for index in range(IMGS)]
    return jnp.stack(columns, axis=1).astype(jnp.int32)


def block_scale(own_key, shape, cuts, least, largest):
    gain = 1.0
    for axis_at, parts in cuts:
        steps = jax.random.uniform(jax.random.fold_in(jax.random.fold_in(own_key, 6), axis_at), (parts,), jnp.float32, least / len(cuts), largest / len(cuts))
        gain = gain * jnp.repeat(jnp.exp(steps), shape[axis_at] // parts).reshape((-1,) + (1,) * (len(shape) - 1 - axis_at))
    return gain


def normal_values(stream_key, shape, scale, bound, pieces=(), kind=jnp.bfloat16):
    values = scale * jax.random.normal(stream_key, shape, jnp.float32)
    if pieces:
        values = values * block_scale(stream_key, shape, pieces, -0.22, 0.18)
    return jnp.clip(values, -bound, bound).astype(kind)


def setup_inputs(seed: int = 0, part: int = 0) -> dict:
    seeds = jax.random.split(jax.random.key(seed), 7)
    own_keys = jax.random.split(jax.random.fold_in(seeds[6], part), 7)
    query_rows = draw_query_rows(jax.random.fold_in(jax.random.fold_in(seeds[6], part), 71), part)
    key_rows = draw_key_rows(jax.random.fold_in(jax.random.fold_in(seeds[6], part), 71), part)
    value_rows = normal_values(own_keys[2], (TOKENS, D), 1.0, 6.0, ((0, 16),))
    grad_hosted = normal_values(own_keys[3], (HOSTED, D), 1.0, 6.0, ((0, 16),))
    image_grid = draw_image_grid(jax.random.fold_in(jax.random.fold_in(seeds[6], part), 71), part)
    destination = draw_destination(jax.random.fold_in(jax.random.fold_in(seeds[6], part), 71), part)
    return {"query_rows": query_rows, "key_rows": key_rows, "value_rows": value_rows, "grad_hosted": grad_hosted, "image_grid": image_grid, "destination": destination}


def attend_exact(query_blk, key_blk, value_blk, grad_blk, row_keys):
    inv_root = HEAD_DIM ** -0.5
    query_float = query_blk.astype(jnp.float32)
    key_float = key_blk.astype(jnp.float32)
    value_float = value_blk.astype(jnp.float32)
    grad_float = grad_blk.astype(jnp.float32)
    scores = jnp.einsum("qhd,khd->hqk", query_float, key_float) * inv_root
    allowed = (row_keys[:, None] == row_keys[None, :]) & (row_keys[None, :] >= 0)
    scores = jnp.where(allowed[None], scores, -1e30)
    row_max = jnp.max(scores, axis=2, keepdims=True)
    weights = jnp.exp(scores - row_max)
    probabilities = weights / jnp.sum(weights, axis=2, keepdims=True)
    probabilities = jnp.where((row_keys >= 0)[None, :, None], probabilities, 0.0)
    probs_bf = lax.optimization_barrier(probabilities.astype(jnp.bfloat16)).astype(jnp.float32)
    attended = jnp.einsum("hqk,khd->qhd", probs_bf, value_float).astype(jnp.bfloat16)
    attended_float = lax.optimization_barrier(attended).astype(jnp.float32)
    grad_probs = jnp.einsum("qhd,khd->hqk", grad_float, value_float)
    row_dot = jnp.sum(grad_float * attended_float, axis=2)
    grad_scores = (probabilities * (grad_probs - jnp.transpose(row_dot)[:, :, None]) * inv_root).astype(jnp.bfloat16)
    grad_scores = lax.optimization_barrier(grad_scores).astype(jnp.float32)
    grad_query = jnp.einsum("hqk,khd->qhd", grad_scores, key_float).astype(jnp.bfloat16)
    grad_key = jnp.einsum("hqk,qhd->khd", grad_scores, query_float).astype(jnp.bfloat16)
    grad_value = jnp.einsum("hqk,qhd->khd", probs_bf, grad_float).astype(jnp.bfloat16)
    return attended, grad_query, grad_key, grad_value


def reference(query_rows, key_rows, value_rows, grad_hosted, image_grid, destination):
    lengths = (image_grid[:, :, 0] * image_grid[:, :, 1]).astype(jnp.int32)
    starts = (jnp.cumsum(lengths, axis=1) - lengths).astype(jnp.int32)
    rank_ids = jnp.arange(N_DP, dtype=jnp.int32)
    image_ids = jnp.arange(IMGS, dtype=jnp.int32)
    source = jnp.sum(jnp.where(destination[None, :, :] == rank_ids[:, None, None], rank_ids[None, :, None], 0), axis=1).astype(jnp.int32)
    grad_slots = grad_hosted.reshape(N_DP, IMGS, MAXLEN, D)

    def one_rank(rank):
        start_row = (rank * RANK_ROWS).astype(jnp.int32)
        query_part = lax.dynamic_slice_in_dim(query_rows, start_row, RANK_ROWS, 0)
        key_part = lax.dynamic_slice_in_dim(key_rows, start_row, RANK_ROWS, 0)
        value_part = lax.dynamic_slice_in_dim(value_rows, start_row, RANK_ROWS, 0)
        own_lengths = lengths[rank]
        own_starts = starts[rank]
        own_dest = destination[rank]
        row_ids = jnp.arange(RANK_ROWS, dtype=jnp.int32)
        image_of = (jnp.sum((own_starts[None, :] <= row_ids[:, None]).astype(jnp.int32), axis=1) - 1).astype(jnp.int32)
        is_live = row_ids < jnp.sum(own_lengths)
        row_keys = jnp.where(is_live, image_of, -1).astype(jnp.int32)
        host_rank = own_dest[image_of].astype(jnp.int32)
        offset = jnp.where(is_live, row_ids - own_starts[image_of], 0).astype(jnp.int32)
        grad_part = jnp.where(is_live[:, None], grad_slots[host_rank, image_of, offset], jnp.zeros((), grad_hosted.dtype))
        shape = (RANK_ROWS, HEADS, HEAD_DIM)
        attended, grad_q, grad_k, grad_v = attend_exact(query_part.reshape(shape), key_part.reshape(shape), value_part.reshape(shape), grad_part.reshape(shape), row_keys)
        return attended.reshape(RANK_ROWS, D), grad_q.reshape(RANK_ROWS, D), grad_k.reshape(RANK_ROWS, D), grad_v.reshape(RANK_ROWS, D)

    attended_all, grad_q_all, grad_k_all, grad_v_all = lax.map(one_rank, rank_ids)
    source_start = starts[source, image_ids[None, :]].astype(jnp.int32)
    source_length = lengths[source, image_ids[None, :]].astype(jnp.int32)
    offsets = jnp.arange(MAXLEN, dtype=jnp.int32)
    source_row = jnp.clip(source_start[:, :, None] + offsets[None, None, :], 0, RANK_ROWS - 1).astype(jnp.int32)
    picked = attended_all[source[:, :, None], source_row]
    in_slot = offsets[None, None, :] < source_length[:, :, None]
    hosted_out = jnp.where(in_slot[:, :, :, None], picked, jnp.zeros((), picked.dtype)).reshape(HOSTED, D)
    return hosted_out, grad_q_all.reshape(TOKENS, D), grad_k_all.reshape(TOKENS, D), grad_v_all.reshape(TOKENS, D)
```

```python
import functools

import jax
import jax.numpy as jnp
from jax import lax
from jax.experimental import pallas as pl
from jax.experimental.pallas import tpu as pltpu
from jax.sharding import PartitionSpec as P

HEAD_DIM = 80
VMEM_BYTES = 48 * 1024 * 1024


def image_place(grid_ref, rank, slot):
    start = jnp.int32(0)
    length = jnp.int32(0)
    for image in range(grid_ref.shape[1]):
        patches = grid_ref[rank, image, 0] * grid_ref[rank, image, 1]
        start = start + jnp.where(image < slot, patches, 0)
        length = jnp.where(image == slot, patches, length)
    return start, length


def row_pick(slot_rows, part_rows, first, start, length, transposed=False):
    shape = (part_rows, slot_rows) if transposed else (slot_rows, part_rows)
    offset = lax.broadcasted_iota(jnp.int32, shape, 1 if transposed else 0)
    row = lax.broadcasted_iota(jnp.int32, shape, 0 if transposed else 1) + first
    return jnp.where((row == start + offset) & (offset < length), 1.0, 0.0).astype(jnp.bfloat16)


def dot(a, b, a_dim, b_dim):
    return lax.dot_general(
        a, b, (((a_dim,), (b_dim,)), ((), ())), preferred_element_type=jnp.float32
    )


def forward_kernel(
    grid_ref, q_own, q_far, k_own, k_far, v_own, v_far, q_img, k_img, v_img, out_ref, lse_ref
):
    rank = lax.axis_index("dp")
    slot = lax.axis_index("seq")
    start, length = image_place(grid_ref, rank, slot)
    slot_rows, width = out_ref.shape
    part_rows = q_own.shape[0]
    heads = width // HEAD_DIM
    inv_root = HEAD_DIM**-0.5
    pick_own = row_pick(slot_rows, part_rows, slot * part_rows, start, length)
    pick_far = row_pick(slot_rows, part_rows, (1 - slot) * part_rows, start, length)
    for own, far, image in ((q_own, q_far, q_img), (k_own, k_far, k_img), (v_own, v_far, v_img)):
        image[...] = (dot(pick_own, own[...], 1, 0) + dot(pick_far, far[...], 1, 0)).astype(
            image.dtype
        )
    key_ids = lax.broadcasted_iota(jnp.int32, (1, slot_rows), 1)
    key_bias = jnp.where(key_ids < length, 0.0, -1e30)
    row_ids = lax.broadcasted_iota(jnp.int32, (slot_rows, 1), 0)
    live = row_ids < length
    lane = lax.broadcasted_iota(jnp.int32, lse_ref.shape, 1)
    lse_all = jnp.zeros(lse_ref.shape, jnp.float32)
    for head in range(heads):
        cols = slice(head * HEAD_DIM, (head + 1) * HEAD_DIM)
        scores = dot(q_img[:, cols], k_img[:, cols], 1, 1) * inv_root + key_bias
        row_max = jnp.max(scores, axis=1, keepdims=True)
        weights = jnp.exp(scores - row_max)
        total = jnp.sum(weights, axis=1, keepdims=True)
        probs = (weights * (1.0 / total)).astype(jnp.bfloat16)
        attended = dot(probs, v_img[:, cols], 1, 0)
        out_ref[:, cols] = jnp.where(live, attended, 0.0).astype(out_ref.dtype)
        lse_all = jnp.where(lane == head, row_max + jnp.log(total), lse_all)
    lse_ref[...] = lse_all


def backward_kernel(
    grid_ref, q_img, k_img, v_img, out_ref, lse_ref, g_ref, *outs_and_scratch
):
    own_refs = outs_and_scratch[:3]
    far_refs = outs_and_scratch[3:6]
    g_img, dq_img, dk_img, dv_img = outs_and_scratch[6:]
    rank = lax.axis_index("dp")
    slot = lax.axis_index("seq")
    start, length = image_place(grid_ref, rank, slot)
    slot_rows, width = out_ref.shape
    part_rows = own_refs[0].shape[0]
    heads = width // HEAD_DIM
    inv_root = HEAD_DIM**-0.5
    row_ids = lax.broadcasted_iota(jnp.int32, (slot_rows, 1), 0)
    live = row_ids < length
    g_rows = g_ref[...].reshape(slot_rows, width)
    g_img[...] = jnp.where(live, g_rows, jnp.zeros_like(g_rows))
    key_ids = lax.broadcasted_iota(jnp.int32, (1, slot_rows), 1)
    key_bias = jnp.where(key_ids < length, 0.0, -1e30)
    for head in range(heads):
        cols = slice(head * HEAD_DIM, (head + 1) * HEAD_DIM)
        q, k, v, g = q_img[:, cols], k_img[:, cols], v_img[:, cols], g_img[:, cols]
        scores = dot(q, k, 1, 1) * inv_root + key_bias
        probs = jnp.exp(scores - lse_ref[:, head : head + 1])
        probs_bf = probs.astype(jnp.bfloat16)
        grad_probs = dot(g, v, 1, 1)
        row_dot = jnp.sum(
            g.astype(jnp.float32) * out_ref[:, cols].astype(jnp.float32), axis=1, keepdims=True
        )
        grad_scores = (probs * (grad_probs - row_dot) * inv_root).astype(jnp.bfloat16)
        dq_img[:, cols] = dot(grad_scores, k, 1, 0).astype(dq_img.dtype)
        dk_img[:, cols] = dot(grad_scores, q, 0, 0).astype(dk_img.dtype)
        dv_img[:, cols] = dot(probs_bf, g, 0, 0).astype(dv_img.dtype)
    put_own = row_pick(slot_rows, part_rows, slot * part_rows, start, length, True)
    put_far = row_pick(slot_rows, part_rows, (1 - slot) * part_rows, start, length, True)
    for image, own, far in zip((dq_img, dk_img, dv_img), own_refs, far_refs):
        own[...] = dot(put_own, image[...], 1, 0).astype(own.dtype)
        far[...] = dot(put_far, image[...], 1, 0).astype(far.dtype)


def middle_kernel(dest_ref, g_ref, o_ref, out_ref, g_sem, o_sem):
    slot = lax.axis_index("seq")
    ranks, block = g_ref.shape[:2]
    copies = []
    for rank in range(ranks):
        copies.append(
            pltpu.make_async_copy(
                g_ref.at[dest_ref[rank, slot]], out_ref.at[rank, pl.ds(0, block)], g_sem.at[rank]
            )
        )
        copies.append(
            pltpu.make_async_copy(
                o_ref.at[pl.ds(rank * block, block)],
                out_ref.at[rank, pl.ds(block, block)],
                o_sem.at[rank],
            )
        )
    for copy in copies:
        copy.start()
    for copy in copies:
        copy.wait()


def last_kernel(dest_ref, in_ref, out_ref, sem):
    slot = lax.axis_index("seq")
    ranks, block = out_ref.shape[:2]
    copies = []
    for rank in range(ranks):
        copies.append(
            pltpu.make_async_copy(
                in_ref.at[rank, pl.ds(block, block)], out_ref.at[dest_ref[rank, slot]], sem.at[rank]
            )
        )
    for copy in copies:
        copy.start()
    for copy in copies:
        copy.wait()


SMEM = pl.BlockSpec(memory_space=pltpu.SMEM)
VMEM = pl.BlockSpec(memory_space=pltpu.VMEM)
ANY = pl.BlockSpec(memory_space=pl.ANY)


def bf16(*shape):
    return jax.ShapeDtypeStruct(shape, jnp.bfloat16)


def local(query_rows, key_rows, value_rows, grad_hosted, image_grid, destination):
    ranks = lax.axis_size("dp")
    slot = lax.axis_index("seq")
    part_rows, width = query_rows.shape
    slot_rows = grad_hosted.shape[0]
    heads = width // HEAD_DIM
    block = slot_rows // ranks
    by_kernel = block % 16 == 0
    flops = 2 * slot_rows * slot_rows * width
    params = pltpu.CompilerParams(vmem_limit_bytes=VMEM_BYTES)

    def swap(x):
        return lax.ppermute(x, "seq", [(0, 1), (1, 0)])

    def spread(x):
        return lax.all_to_all(x, "dp", 0, 0, tiled=True)

    grad_spread = spread(grad_hosted.reshape(ranks, block, width))

    pairs = []
    for rows in (query_rows, key_rows, value_rows):
        pairs += [rows, swap(rows)]
    q_img, k_img, v_img, attended, lse = pl.pallas_call(
        forward_kernel,
        out_shape=[bf16(slot_rows, width)] * 4
        + [jax.ShapeDtypeStruct((slot_rows, 128), jnp.float32)],
        in_specs=[SMEM] + [VMEM] * 6,
        out_specs=[VMEM] * 5,
        compiler_params=params,
        cost_estimate=pl.CostEstimate(
            flops=5 * flops, bytes_accessed=6 * 2 * slot_rows * width, transcendentals=slot_rows * slot_rows * heads
        ),
        name="attend",
    )(image_grid, *pairs)

    if by_kernel:
        both = pl.pallas_call(
            middle_kernel,
            out_shape=bf16(ranks, 2 * block, width),
            in_specs=[SMEM, ANY, ANY],
            out_specs=ANY,
            scratch_shapes=[pltpu.SemaphoreType.DMA((ranks,)), pltpu.SemaphoreType.DMA((ranks,))],
            name="order_by_lister",
        )(destination, grad_spread, attended)
    else:
        dest = lax.dynamic_index_in_dim(destination, slot, 1, keepdims=False)
        both = jnp.concatenate(
            [grad_spread[dest], attended.reshape(ranks, block, width)], axis=1
        )
    both = spread(both)

    if by_kernel:
        host_order = pl.pallas_call(
            last_kernel,
            out_shape=bf16(ranks, block, width),
            in_specs=[SMEM, ANY],
            out_specs=ANY,
            scratch_shapes=[pltpu.SemaphoreType.DMA((ranks,))],
            name="order_by_host",
        )(destination, both)
        grad_slot = both
        grad_spec = pl.BlockSpec((ranks, block, width), lambda i: (0, 0, 0))
    else:
        rank_ids = jnp.arange(ranks, dtype=jnp.int32)
        source = jnp.sum(
            jnp.where(dest[None, :] == rank_ids[:, None], rank_ids[None, :], 0), axis=1
        )
        host_order = both[source, block:]
        grad_slot = both[:, :block].reshape(1, slot_rows, width)
        grad_spec = pl.BlockSpec((1, slot_rows, width), lambda i: (0, 0, 0))
    hosted_out = spread(host_order).reshape(slot_rows, width)

    def whole(*shape):
        return pl.BlockSpec(shape, lambda i: (0,) * len(shape))

    grads = pl.pallas_call(
        backward_kernel,
        grid=(1,),
        out_shape=[bf16(part_rows, width)] * 6,
        in_specs=[SMEM]
        + [whole(slot_rows, width)] * 4
        + [whole(slot_rows, 128), grad_spec],
        out_specs=[whole(part_rows, width)] * 6,
        scratch_shapes=[pltpu.VMEM((slot_rows, width), jnp.bfloat16)] * 4,
        compiler_params=params,
        cost_estimate=pl.CostEstimate(
            flops=9 * flops, bytes_accessed=11 * 2 * slot_rows * width, transcendentals=slot_rows * slot_rows * heads
        ),
        name="attend_back",
    )(image_grid, q_img, k_img, v_img, attended, lse, grad_slot)
    grad_query, grad_key, grad_value = (
        own + swap(far) for own, far in zip(grads[:3], grads[3:])
    )
    return hosted_out, grad_query, grad_key, grad_value


def solution(mesh):
    rows = P(("groups", "dp", "seq"), None)
    return jax.shard_map(
        local,
        mesh=mesh,
        in_specs=(rows, rows, rows, rows, P("groups", None, None), P("groups", None)),
        out_specs=(rows,) * 4,
        check_vma=False,
    )
```

```python
import jax
import jax.numpy as jnp
from jax import lax
from jax.experimental import pallas as pl
from jax.experimental.pallas import tpu as pltpu
from jax.sharding import PartitionSpec as P

HEAD_DIM = 80
VMEM_BYTES = 48 * 1024 * 1024


def image_place(grid_ref, rank, slot):
    start = jnp.int32(0)
    length = jnp.int32(0)
    for image in range(grid_ref.shape[1]):
        patches = grid_ref[rank, image, 0] * grid_ref[rank, image, 1]
        start = start + jnp.where(image < slot, patches, 0)
        length = jnp.where(image == slot, patches, length)
    return start, length


def row_pick(slot_rows, part_rows, first, start, length, transposed=False):
    shape = (part_rows, slot_rows) if transposed else (slot_rows, part_rows)
    offset = lax.broadcasted_iota(jnp.int32, shape, 1 if transposed else 0)
    row = lax.broadcasted_iota(jnp.int32, shape, 0 if transposed else 1) + first
    return jnp.where((row == start + offset) & (offset < length), 1.0, 0.0).astype(jnp.bfloat16)


def dot(a, b, a_dim, b_dim):
    return lax.dot_general(
        a, b, (((a_dim,), (b_dim,)), ((), ())), preferred_element_type=jnp.float32
    )


def forward_kernel(
    grid_ref, q_own, q_far, k_own, k_far, v_own, v_far, q_img, k_img, v_img, out_ref, lse_ref
):
    rank = lax.axis_index("dp")
    slot = lax.axis_index("seq")
    start, length = image_place(grid_ref, rank, slot)
    slot_rows, width = out_ref.shape
    part_rows = q_own.shape[0]
    heads = width // HEAD_DIM
    inv_root = HEAD_DIM**-0.5
    pick_own = row_pick(slot_rows, part_rows, slot * part_rows, start, length)
    pick_far = row_pick(slot_rows, part_rows, (1 - slot) * part_rows, start, length)
    for own, far, image in ((q_own, q_far, q_img), (k_own, k_far, k_img), (v_own, v_far, v_img)):
        image[...] = (dot(pick_own, own[...], 1, 0) + dot(pick_far, far[...], 1, 0)).astype(
            image.dtype
        )
    key_ids = lax.broadcasted_iota(jnp.int32, (1, slot_rows), 1)
    key_bias = jnp.where(key_ids < length, 0.0, -1e30)
    row_ids = lax.broadcasted_iota(jnp.int32, (slot_rows, 1), 0)
    live = row_ids < length
    lane = lax.broadcasted_iota(jnp.int32, lse_ref.shape, 1)
    lse_all = jnp.zeros(lse_ref.shape, jnp.float32)
    for head in range(heads):
        cols = slice(head * HEAD_DIM, (head + 1) * HEAD_DIM)
        scores = dot(q_img[:, cols], k_img[:, cols], 1, 1) * inv_root + key_bias
        row_max = jnp.max(scores, axis=1, keepdims=True)
        weights = jnp.exp(scores - row_max)
        total = jnp.sum(weights, axis=1, keepdims=True)
        probs = (weights * (1.0 / total)).astype(jnp.bfloat16)
        attended = dot(probs, v_img[:, cols], 1, 0)
        out_ref[:, cols] = jnp.where(live, attended, 0.0).astype(out_ref.dtype)
        lse_all = jnp.where(lane == head, row_max + jnp.log(total), lse_all)
    lse_ref[...] = lse_all


def backward_kernel(
    grid_ref, q_img, k_img, v_img, out_ref, lse_ref, g_ref, *outs_and_scratch
):
    own_refs = outs_and_scratch[:3]
    far_refs = outs_and_scratch[3:6]
    g_img, dq_img, dk_img, dv_img = outs_and_scratch[6:]
    rank = lax.axis_index("dp")
    slot = lax.axis_index("seq")
    start, length = image_place(grid_ref, rank, slot)
    slot_rows, width = out_ref.shape
    part_rows = own_refs[0].shape[0]
    heads = width // HEAD_DIM
    inv_root = HEAD_DIM**-0.5
    row_ids = lax.broadcasted_iota(jnp.int32, (slot_rows, 1), 0)
    live = row_ids < length
    g_rows = g_ref[...].reshape(slot_rows, width)
    g_img[...] = jnp.where(live, g_rows, jnp.zeros_like(g_rows))
    key_ids = lax.broadcasted_iota(jnp.int32, (1, slot_rows), 1)
    key_bias = jnp.where(key_ids < length, 0.0, -1e30)
    for head in range(heads):
        cols = slice(head * HEAD_DIM, (head + 1) * HEAD_DIM)
        q, k, v, g = q_img[:, cols], k_img[:, cols], v_img[:, cols], g_img[:, cols]
        scores = dot(q, k, 1, 1) * inv_root + key_bias
        probs = jnp.exp(scores - lse_ref[:, head : head + 1])
        probs_bf = probs.astype(jnp.bfloat16)
        grad_probs = dot(g, v, 1, 1)
        row_dot = jnp.sum(
            g.astype(jnp.float32) * out_ref[:, cols].astype(jnp.float32), axis=1, keepdims=True
        )
        grad_scores = (probs * (grad_probs - row_dot) * inv_root).astype(jnp.bfloat16)
        dq_img[:, cols] = dot(grad_scores, k, 1, 0).astype(dq_img.dtype)
        dk_img[:, cols] = dot(grad_scores, q, 0, 0).astype(dk_img.dtype)
        dv_img[:, cols] = dot(probs_bf, g, 0, 0).astype(dv_img.dtype)
    put_own = row_pick(slot_rows, part_rows, slot * part_rows, start, length, True)
    put_far = row_pick(slot_rows, part_rows, (1 - slot) * part_rows, start, length, True)
    for image, own, far in zip((dq_img, dk_img, dv_img), own_refs, far_refs):
        own[...] = dot(put_own, image[...], 1, 0).astype(own.dtype)
        far[...] = dot(put_far, image[...], 1, 0).astype(far.dtype)


def middle_kernel(dest_ref, g_ref, o_ref, out_ref):
    slot = lax.axis_index("seq")
    ranks, block = g_ref.shape[:2]
    for rank in range(ranks):
        out_ref[rank, :block] = g_ref[dest_ref[rank, slot]]
        out_ref[rank, block:] = o_ref[rank * block : (rank + 1) * block]


def last_kernel(dest_ref, in_ref, out_ref):
    slot = lax.axis_index("seq")
    for rank in range(out_ref.shape[0]):
        out_ref[dest_ref[rank, slot]] = in_ref[rank]


SMEM = pl.BlockSpec(memory_space=pltpu.SMEM)
VMEM = pl.BlockSpec(memory_space=pltpu.VMEM)


def bf16(*shape):
    return jax.ShapeDtypeStruct(shape, jnp.bfloat16)


def local(query_rows, key_rows, value_rows, grad_hosted, image_grid, destination):
    ranks = lax.axis_size("dp")
    slot = lax.axis_index("seq")
    part_rows, width = query_rows.shape
    slot_rows = grad_hosted.shape[0]
    heads = width // HEAD_DIM
    block = slot_rows // ranks
    by_kernel = block % 16 == 0
    flops = 2 * slot_rows * slot_rows * width
    params = pltpu.CompilerParams(vmem_limit_bytes=VMEM_BYTES)

    def swap(x):
        return lax.ppermute(x, "seq", [(0, 1), (1, 0)])

    def spread(x):
        return lax.all_to_all(x, "dp", 0, 0, tiled=True)

    grad_spread = spread(grad_hosted.reshape(ranks, block, width))

    pairs = []
    for rows in (query_rows, key_rows, value_rows):
        pairs += [rows, swap(rows)]
    q_img, k_img, v_img, attended, lse = pl.pallas_call(
        forward_kernel,
        out_shape=[bf16(slot_rows, width)] * 4
        + [jax.ShapeDtypeStruct((slot_rows, 128), jnp.float32)],
        in_specs=[SMEM] + [VMEM] * 6,
        out_specs=[VMEM] * 5,
        compiler_params=params,
        cost_estimate=pl.CostEstimate(
            flops=5 * flops, bytes_accessed=6 * 2 * slot_rows * width, transcendentals=slot_rows * slot_rows * heads
        ),
        name="attend",
    )(image_grid, *pairs)

    if by_kernel:
        both = pl.pallas_call(
            middle_kernel,
            out_shape=bf16(ranks, 2 * block, width),
            in_specs=[SMEM, VMEM, VMEM],
            out_specs=VMEM,
            name="order_by_lister",
        )(destination, grad_spread, attended)
    else:
        dest = lax.dynamic_index_in_dim(destination, slot, 1, keepdims=False)
        both = jnp.concatenate(
            [grad_spread[dest], attended.reshape(ranks, block, width)], axis=1
        )
    both = spread(both)

    if by_kernel:
        host_order = pl.pallas_call(
            last_kernel,
            grid=(1,),
            out_shape=bf16(ranks, block, width),
            in_specs=[SMEM, pl.BlockSpec((ranks, block, width), lambda i: (0, 1, 0))],
            out_specs=pl.BlockSpec((ranks, block, width), lambda i: (0, 0, 0)),
            name="order_by_host",
        )(destination, both)
        grad_slot = both
        grad_spec = pl.BlockSpec((ranks, block, width), lambda i: (0, 0, 0))
    else:
        rank_ids = jnp.arange(ranks, dtype=jnp.int32)
        source = jnp.sum(
            jnp.where(dest[None, :] == rank_ids[:, None], rank_ids[None, :], 0), axis=1
        )
        host_order = both[source, block:]
        grad_slot = both[:, :block].reshape(1, slot_rows, width)
        grad_spec = pl.BlockSpec((1, slot_rows, width), lambda i: (0, 0, 0))
    hosted_out = spread(host_order).reshape(slot_rows, width)

    def whole(*shape):
        return pl.BlockSpec(shape, lambda i: (0,) * len(shape))

    grads = pl.pallas_call(
        backward_kernel,
        grid=(1,),
        out_shape=[bf16(part_rows, width)] * 6,
        in_specs=[SMEM]
        + [whole(slot_rows, width)] * 4
        + [whole(slot_rows, 128), grad_spec],
        out_specs=[whole(part_rows, width)] * 6,
        scratch_shapes=[pltpu.VMEM((slot_rows, width), jnp.bfloat16)] * 4,
        compiler_params=params,
        cost_estimate=pl.CostEstimate(
            flops=9 * flops, bytes_accessed=11 * 2 * slot_rows * width, transcendentals=slot_rows * slot_rows * heads
        ),
        name="attend_back",
    )(image_grid, q_img, k_img, v_img, attended, lse, grad_slot)
    grad_query, grad_key, grad_value = (
        own + swap(far) for own, far in zip(grads[:3], grads[3:])
    )
    return hosted_out, grad_query, grad_key, grad_value


def solution(mesh):
    rows = P(("groups", "dp", "seq"), None)
    return jax.shard_map(
        local,
        mesh=mesh,
        in_specs=(rows, rows, rows, rows, P("groups", None, None), P("groups", None)),
        out_specs=(rows,) * 4,
        check_vma=False,
    )
```

```python
import jax
import jax.numpy as jnp
from jax import lax
from jax.experimental import pallas as pl
from jax.experimental.pallas import tpu as pltpu
from jax.sharding import PartitionSpec as P


HEAD_DIM = 80
STRIP = 256
STEPS = (0, 7, 1, 2, 5, 3, 4, 6)
LARGE = pltpu.CompilerParams(vmem_limit_bytes=12 * 1024 * 1024)
SMALL = pltpu.CompilerParams(vmem_limit_bytes=6 * 1024 * 1024)
SMEM = pl.BlockSpec(memory_space=pltpu.SMEM)
VMEM = pl.BlockSpec(memory_space=pltpu.VMEM)
HBM = pl.BlockSpec(memory_space=pltpu.HBM)


def dot(a, b, a_dim, b_dim):
    return lax.dot_general(
        a, b, (((a_dim,), (b_dim,)), ((), ())), preferred_element_type=jnp.float32
    )


def one_hot(condition):
    return jnp.where(condition, 1.0, 0.0).astype(jnp.bfloat16)


def iota(shape, dim):
    return lax.broadcasted_iota(jnp.int32, shape, dim)


def strips(width):
    return [slice(at, at + STRIP) for at in range(0, width, STRIP)]


def length_of(grid_ref, rank, image):
    return grid_ref[image, 0, rank] * grid_ref[image, 1, rank]


def image_place(grid_ref, rank, slot):
    start = jnp.int32(0)
    length = jnp.int32(0)
    for image in range(grid_ref.shape[0]):
        patches = length_of(grid_ref, rank, image)
        start = start + jnp.where(image < slot, patches, 0)
        length = jnp.where(image == slot, patches, length)
    return start, length


def row_pick(slot_rows, part_rows, first, start, length, transposed=False):
    shape = (part_rows, slot_rows) if transposed else (slot_rows, part_rows)
    offset = iota(shape, 1 if transposed else 0)
    row = iota(shape, 0 if transposed else 1) + first
    return one_hot((row == start + offset) & (offset < length))


def eye(n):
    return one_hot(iota((n, n), 0) == iota((n, n), 1))


def turn(identity, block):
    return dot(identity, block, 1, 1)


def block_of(to, rows):
    return pl.ds(pl.multiple_of(to * rows, rows), rows)


def to_lister_kernel(dest_ref, attended_ref, in_ref, *out_refs):
    rank = lax.axis_index("dp")
    slot = lax.axis_index("seq")
    rows = in_ref.shape[1]
    for step, out_ref in zip(STEPS, out_refs):
        out_ref[:rows] = in_ref[dest_ref[slot, rank ^ step]]
        out_ref[rows:] = attended_ref[block_of(rank ^ step, rows), :]


def to_host_kernel(dest_ref, *refs):
    rank = lax.axis_index("dp")
    slot = lax.axis_index("seq")
    in_refs, (out_ref, grad_ref) = refs[:-2], refs[-2:]
    rows = out_ref.shape[1]
    for step, in_ref in zip(STEPS, in_refs):
        out_ref[dest_ref[slot, rank ^ step]] = in_ref[rows:]
        grad_ref[block_of(rank ^ step, rows), :] = in_ref[:rows]


def store_kernel(in_ref, hbm_ref, sems):
    rows = in_ref.shape[1]
    stores = [
        pltpu.make_async_copy(
            in_ref.at[index], hbm_ref.at[pl.ds(index * rows, rows)], sems.at[index]
        )
        for index in range(in_ref.shape[0])
    ]
    for store in stores:
        store.start()
    for store in stores:
        store.wait()


def join_kernel(*refs):
    hbm_refs, vmem_refs, sems = refs[6:9], refs[9:12], refs[12]
    stores = [
        pltpu.make_async_copy(vmem, hbm, sems.at[index])
        for index, (vmem, hbm) in enumerate(zip(vmem_refs, hbm_refs))
    ]
    for own, far, vmem, store in zip(refs[:3], refs[3:6], vmem_refs, stores):
        vmem[...] = own[...] + far[...]
        store.start()
    for store in stores:
        store.wait()


def forward_kernel(grid_ref, *refs):
    rows, (k_img, v_img, qt_ref, ot_ref, lse_ref), refs = refs[:6], refs[6:11], refs[11:]
    out_ref, q_img, vt_ref = refs
    rank = lax.axis_index("dp")
    slot = lax.axis_index("seq")
    start, length = image_place(grid_ref, rank, slot)
    slot_rows, width = k_img.shape
    part_rows = rows[0].shape[0]
    inv_root = HEAD_DIM**-0.5
    pick_own = row_pick(slot_rows, part_rows, slot * part_rows, start, length)
    pick_far = row_pick(slot_rows, part_rows, (1 - slot) * part_rows, start, length)
    for own, far, image in zip(rows[0::2], rows[1::2], (q_img, k_img, v_img)):
        image[...] = (dot(pick_own, own[...], 1, 0) + dot(pick_far, far[...], 1, 0)).astype(
            image.dtype
        )
    identity = eye(slot_rows)
    for part in strips(width):
        qt_ref[part] = turn(identity, q_img[:, part]).astype(qt_ref.dtype)
        vt_ref[part] = turn(identity, v_img[:, part]).astype(vt_ref.dtype)
    key_bias = jnp.where(iota((slot_rows, 1), 0) < length, 0.0, -1e30)
    live = iota((1, slot_rows), 1) < length
    for head in range(width // HEAD_DIM):
        part = slice(head * HEAD_DIM, (head + 1) * HEAD_DIM)
        scores = dot(k_img[:, part], qt_ref[part], 1, 0) * inv_root + key_bias
        top = jnp.max(scores, axis=0, keepdims=True)
        weights = jnp.exp(scores - top)
        total = jnp.sum(weights, axis=0, keepdims=True)
        probs = (weights * jnp.where(live, 1.0 / total, 0.0)).astype(jnp.bfloat16)
        ot_ref[part] = dot(vt_ref[part], probs, 1, 0).astype(ot_ref.dtype)
        lse_ref[head : head + 1] = top + jnp.log(total)
    for part in strips(width):
        out_ref[:, part] = turn(identity, ot_ref[part]).astype(out_ref.dtype)


def backward_kernel(grid_ref, *refs):
    (k_img, v_img, qt_ref, ot_ref, lse_ref), refs = refs[:5], refs[5:]
    g_img, own_refs, far_refs, (gt_ref, kt_ref, *grad_refs) = refs[0], refs[1:4], refs[4:7], refs[7:]
    rank = lax.axis_index("dp")
    slot = lax.axis_index("seq")
    start, length = image_place(grid_ref, rank, slot)
    slot_rows, width = k_img.shape
    part_rows = own_refs[0].shape[0]
    inv_root = HEAD_DIM**-0.5
    identity = eye(slot_rows)
    live = iota((1, slot_rows), 1) < length
    for part in strips(width):
        gt_ref[part] = jnp.where(live, turn(identity, g_img[:, part]), 0.0).astype(gt_ref.dtype)
        kt_ref[part] = turn(identity, k_img[:, part]).astype(kt_ref.dtype)
    key_bias = jnp.where(iota((slot_rows, 1), 0) < length, 0.0, -1e30)
    dq_ref, dk_ref, dv_ref = grad_refs
    for head in range(width // HEAD_DIM):
        part = slice(head * HEAD_DIM, (head + 1) * HEAD_DIM)
        qt, gt = qt_ref[part], gt_ref[part]
        scores = dot(k_img[:, part], qt, 1, 0) * inv_root + key_bias
        probs = jnp.exp(scores - lse_ref[head : head + 1])
        grad_probs = dot(v_img[:, part], gt, 1, 0)
        row_dot = jnp.sum(
            gt.astype(jnp.float32) * ot_ref[part].astype(jnp.float32), axis=0, keepdims=True
        )
        grad_scores = (probs * (grad_probs - row_dot) * inv_root).astype(jnp.bfloat16)
        dq_ref[part] = dot(kt_ref[part], grad_scores, 1, 0).astype(dq_ref.dtype)
        dk_ref[part] = dot(qt, grad_scores, 1, 1).astype(dk_ref.dtype)
        dv_ref[part] = dot(gt, probs.astype(jnp.bfloat16), 1, 1).astype(dv_ref.dtype)
    put_own = row_pick(slot_rows, part_rows, slot * part_rows, start, length, True)
    put_far = row_pick(slot_rows, part_rows, (1 - slot) * part_rows, start, length, True)
    for grad, own, far in zip(grad_refs, own_refs, far_refs):
        own[...] = dot(put_own, grad[...], 1, 1).astype(own.dtype)
        far[...] = dot(put_far, grad[...], 1, 1).astype(far.dtype)


def bf16(*shape):
    return jax.ShapeDtypeStruct(shape, jnp.bfloat16)


def table(x):
    return jax.ShapeDtypeStruct(x.shape, x.dtype)


def local(query_rows, key_rows, value_rows, grad_hosted, image_grid, destination):
    ranks = lax.axis_size("dp")
    slot = lax.axis_index("seq")
    image_grid = jnp.transpose(image_grid, (1, 2, 0))
    destination = jnp.transpose(destination)
    part_rows, width = query_rows.shape
    slot_rows = grad_hosted.shape[0]
    heads = width // HEAD_DIM
    block = slot_rows // ranks
    by_pairs = ranks == len(STEPS) and block % 16 == 0
    flops = 2 * slot_rows * slot_rows * width
    exps = slot_rows * slot_rows * heads

    def swap(x):
        return lax.ppermute(x, "seq", [(0, 1), (1, 0)])

    def call(kernel, ins, outs, params, name, scratch=(), work=0, out_spec=VMEM, sems=0):
        return pl.pallas_call(
            kernel,
            out_shape=outs,
            in_specs=[SMEM if x.dtype == jnp.int32 else VMEM for x in ins],
            out_specs=[out_spec] * len(outs),
            scratch_shapes=[pltpu.VMEM(shape, jnp.bfloat16) for shape in scratch]
            + [pltpu.SemaphoreType.DMA((sems,))] * (sems > 0),
            compiler_params=params,
            cost_estimate=pl.CostEstimate(
                flops=work * flops + 1,
                bytes_accessed=sum(x.size * x.dtype.itemsize for x in (*ins, *outs)),
                transcendentals=exps if work else 0,
            ),
            name=name,
        )(*ins)

    def spread(x):
        return lax.all_to_all(x, "dp", 0, 0, tiled=True)

    def exchange(blocks):
        return [
            lax.ppermute(x, "dp", [(rank, rank ^ step) for rank in range(ranks)]) if step else x
            for step, x in zip(STEPS, blocks)
        ]

    rows = []
    for x in (query_rows, key_rows, value_rows):
        rows += [x, swap(x)]
    grad_spread = spread(grad_hosted.reshape(ranks, block, width))
    k_img, v_img, q_turned, out_turned, lse, attended = call(
        forward_kernel,
        (image_grid, *rows),
        [bf16(slot_rows, width)] * 2
        + [bf16(width, slot_rows)] * 2
        + [jax.ShapeDtypeStruct((heads, slot_rows), jnp.float32)]
        + [bf16(slot_rows, width)],
        LARGE,
        "attend",
        scratch=[(slot_rows, width), (width, slot_rows)],
        work=2,
    )
    if by_pairs:
        messages = call(
            to_lister_kernel,
            (destination, attended, grad_spread),
            [bf16(2 * block, width)] * ranks,
            SMALL,
            "to_lister",
        )
        host_order, grad_slot = call(
            to_host_kernel,
            (destination, *exchange(messages)),
            [bf16(ranks, block, width), bf16(slot_rows, width)],
            SMALL,
            "to_host",
        )
        (hosted_out,) = call(
            store_kernel,
            (spread(host_order),),
            [bf16(slot_rows, width)],
            SMALL,
            "store",
            out_spec=HBM,
            sems=ranks,
        )
    else:
        dest = lax.dynamic_index_in_dim(destination, slot, 0, keepdims=False)
        rank_ids = jnp.arange(ranks, dtype=jnp.int32)
        source = jnp.sum(
            jnp.where(dest[None, :] == rank_ids[:, None], rank_ids[None, :], 0), axis=1
        )
        both = spread(
            jnp.concatenate([grad_spread[dest], attended.reshape(ranks, block, width)], axis=1)
        )
        grad_slot = both[:, :block].reshape(slot_rows, width)
        hosted_out = spread(both[source, block:]).reshape(slot_rows, width)
    grads = call(
        backward_kernel,
        (image_grid, k_img, v_img, q_turned, out_turned, lse, grad_slot),
        [bf16(part_rows, width)] * 6,
        LARGE,
        "attend_back",
        scratch=[(width, slot_rows)] * 5,
        work=5,
    )
    grad_query, grad_key, grad_value = call(
        join_kernel,
        (*grads[:3], *(swap(x) for x in grads[3:])),
        [bf16(part_rows, width)] * 3,
        SMALL,
        "join",
        scratch=[(part_rows, width)] * 3,
        out_spec=HBM,
        sems=3,
    )
    return hosted_out, grad_query, grad_key, grad_value


def solution(mesh):
    rows = P(("groups", "dp", "seq"), None)
    return jax.shard_map(
        local,
        mesh=mesh,
        in_specs=(rows, rows, rows, rows, P("groups", None, None), P("groups", None)),
        out_specs=(rows,) * 4,
        check_vma=False,
    )
```

```python
import jax
import jax.numpy as jnp
from jax import lax
from jax.experimental import pallas as pl
from jax.experimental.pallas import tpu as pltpu
from jax.sharding import PartitionSpec as P


HEAD_DIM = 80
STRIP = 256
STEPS = (0, 7, 1, 2, 5, 3, 4, 6)
LARGE = pltpu.CompilerParams(vmem_limit_bytes=12 * 1024 * 1024)
SMALL = pltpu.CompilerParams(vmem_limit_bytes=6 * 1024 * 1024)
SMEM = pl.BlockSpec(memory_space=pltpu.SMEM)
VMEM = pl.BlockSpec(memory_space=pltpu.VMEM)
HBM = pl.BlockSpec(memory_space=pltpu.HBM)


def dot(a, b, a_dim, b_dim):
    return lax.dot_general(
        a, b, (((a_dim,), (b_dim,)), ((), ())), preferred_element_type=jnp.float32
    )


def one_hot(condition):
    return jnp.where(condition, 1.0, 0.0).astype(jnp.bfloat16)


def iota(shape, dim):
    return lax.broadcasted_iota(jnp.int32, shape, dim)


def strips(width):
    return [slice(at, at + STRIP) for at in range(0, width, STRIP)]


def length_of(grid_ref, rank, image):
    return grid_ref[image, 0, rank] * grid_ref[image, 1, rank]


def image_place(grid_ref, rank, slot):
    start = jnp.int32(0)
    length = jnp.int32(0)
    for image in range(grid_ref.shape[0]):
        patches = length_of(grid_ref, rank, image)
        start = start + jnp.where(image < slot, patches, 0)
        length = jnp.where(image == slot, patches, length)
    return start, length


def row_pick(slot_rows, part_rows, first, start, length, transposed=False):
    shape = (part_rows, slot_rows) if transposed else (slot_rows, part_rows)
    offset = iota(shape, 1 if transposed else 0)
    row = iota(shape, 0 if transposed else 1) + first
    return one_hot((row == start + offset) & (offset < length))


def eye(n):
    return one_hot(iota((n, n), 0) == iota((n, n), 1))


def turn(identity, block):
    return dot(identity, block, 1, 1)


def block_of(to, rows):
    return pl.ds(pl.multiple_of(to * rows, rows), rows)


def to_lister_kernel(dest_ref, in_ref, *out_refs):
    rank = lax.axis_index("dp")
    slot = lax.axis_index("seq")
    for step, out_ref in zip(STEPS, out_refs):
        out_ref[...] = in_ref[dest_ref[slot, rank ^ step]]


def to_host_kernel(dest_ref, *refs):
    rank = lax.axis_index("dp")
    slot = lax.axis_index("seq")
    count = len(STEPS)
    out_ref, grad_ref = refs[-2:]
    rows = out_ref.shape[1]
    for step, o_ref, g_ref in zip(STEPS, refs[:count], refs[count : 2 * count]):
        out_ref[dest_ref[slot, rank ^ step]] = o_ref[...]
        grad_ref[block_of(rank ^ step, rows), :] = g_ref[...]


def store_kernel(in_ref, hbm_ref, sems):
    rows = in_ref.shape[1]
    stores = [
        pltpu.make_async_copy(
            in_ref.at[index], hbm_ref.at[pl.ds(index * rows, rows)], sems.at[index]
        )
        for index in range(in_ref.shape[0])
    ]
    for store in stores:
        store.start()
    for store in stores:
        store.wait()


def join_kernel(*refs):
    hbm_refs, vmem_refs, sems = refs[6:9], refs[9:12], refs[12]
    stores = [
        pltpu.make_async_copy(vmem, hbm, sems.at[index])
        for index, (vmem, hbm) in enumerate(zip(vmem_refs, hbm_refs))
    ]
    for own, far, vmem, store in zip(refs[:3], refs[3:6], vmem_refs, stores):
        vmem[...] = own[...] + far[...]
        store.start()
    for store in stores:
        store.wait()


def forward_kernel(grid_ref, *refs):
    rows, (k_img, v_img, qt_ref, ot_ref, lse_ref), refs = refs[:6], refs[6:11], refs[11:]
    out_refs, (q_img, vt_ref, out_rows) = refs[:-3], refs[-3:]
    rank = lax.axis_index("dp")
    slot = lax.axis_index("seq")
    start, length = image_place(grid_ref, rank, slot)
    slot_rows, width = k_img.shape
    part_rows = rows[0].shape[0]
    inv_root = HEAD_DIM**-0.5
    pick_own = row_pick(slot_rows, part_rows, slot * part_rows, start, length)
    pick_far = row_pick(slot_rows, part_rows, (1 - slot) * part_rows, start, length)
    for own, far, image in zip(rows[0::2], rows[1::2], (q_img, k_img, v_img)):
        image[...] = (dot(pick_own, own[...], 1, 0) + dot(pick_far, far[...], 1, 0)).astype(
            image.dtype
        )
    identity = eye(slot_rows)
    for part in strips(width):
        qt_ref[part] = turn(identity, q_img[:, part]).astype(qt_ref.dtype)
        vt_ref[part] = turn(identity, v_img[:, part]).astype(vt_ref.dtype)
    key_bias = jnp.where(iota((slot_rows, 1), 0) < length, 0.0, -1e30)
    live = iota((1, slot_rows), 1) < length
    parts = [slice(at, at + HEAD_DIM) for at in range(0, width, HEAD_DIM)]
    raws = {}
    late = []

    def finish():
        part, probs = late.pop(0)
        ot_ref[part] = dot(vt_ref[part], probs, 1, 0).astype(ot_ref.dtype)

    for head, part in enumerate(parts):
        for other in range(head, min(head + 1 + 2, len(parts))):
            if other not in raws:
                raws[other] = dot(k_img[:, parts[other]], qt_ref[parts[other]], 1, 0)
        if len(late) > 1:
            finish()
        scores = raws[head] * inv_root + key_bias
        top = jnp.max(scores, axis=0, keepdims=True)
        weights = jnp.exp(scores - top)
        total = jnp.sum(weights, axis=0, keepdims=True)
        probs = (weights * jnp.where(live, 1.0 / total, 0.0)).astype(jnp.bfloat16)
        lse_ref[head : head + 1] = top + jnp.log(total)
        late.append((part, probs))
    while late:
        finish()
    for part in strips(width):
        out_rows[:, part] = turn(identity, ot_ref[part]).astype(out_rows.dtype)
    if len(out_refs) > 1:
        for step, out_ref in zip(STEPS, out_refs):
            out_ref[...] = out_rows[block_of(rank ^ step, out_ref.shape[0]), :]
    else:
        out_refs[0][...] = out_rows[...]


def backward_kernel(grid_ref, *refs):
    (k_img, v_img, qt_ref, ot_ref, lse_ref), refs = refs[:5], refs[5:]
    g_img, own_refs, far_refs, (gt_ref, kt_ref, *grad_refs) = refs[0], refs[1:4], refs[4:7], refs[7:]
    rank = lax.axis_index("dp")
    slot = lax.axis_index("seq")
    start, length = image_place(grid_ref, rank, slot)
    slot_rows, width = k_img.shape
    part_rows = own_refs[0].shape[0]
    inv_root = HEAD_DIM**-0.5
    identity = eye(slot_rows)
    live = iota((1, slot_rows), 1) < length
    for part in strips(width):
        gt_ref[part] = jnp.where(live, turn(identity, g_img[:, part]), 0.0).astype(gt_ref.dtype)
        kt_ref[part] = turn(identity, k_img[:, part]).astype(kt_ref.dtype)
    key_bias = jnp.where(iota((slot_rows, 1), 0) < length, 0.0, -1e30)
    dq_ref, dk_ref, dv_ref = grad_refs
    parts = [slice(at, at + HEAD_DIM) for at in range(0, width, HEAD_DIM)]
    raws = {}
    late = []

    def finish():
        part, probs, grad_scores = late.pop(0)
        dq_ref[part] = dot(kt_ref[part], grad_scores, 1, 0).astype(dq_ref.dtype)
        dk_ref[part] = dot(qt_ref[part], grad_scores, 1, 1).astype(dk_ref.dtype)
        dv_ref[part] = dot(gt_ref[part], probs, 1, 1).astype(dv_ref.dtype)

    for head, part in enumerate(parts):
        for other in range(head, min(head + 1 + 1, len(parts))):
            if other not in raws:
                at = parts[other]
                raws[other] = (dot(k_img[:, at], qt_ref[at], 1, 0), dot(v_img[:, at], gt_ref[at], 1, 0))
        if len(late) > 0:
            finish()
        raw, grad_probs = raws.pop(head)
        raws[head] = None
        probs = jnp.exp(raw * inv_root + key_bias - lse_ref[head : head + 1])
        row_dot = jnp.sum(
            gt_ref[part].astype(jnp.float32) * ot_ref[part].astype(jnp.float32), axis=0, keepdims=True
        )
        grad_scores = (probs * (grad_probs - row_dot) * inv_root).astype(jnp.bfloat16)
        late.append((part, probs.astype(jnp.bfloat16), grad_scores))
    while late:
        finish()
    put_own = row_pick(slot_rows, part_rows, slot * part_rows, start, length, True)
    put_far = row_pick(slot_rows, part_rows, (1 - slot) * part_rows, start, length, True)
    for grad, own, far in zip(grad_refs, own_refs, far_refs):
        own[...] = dot(put_own, grad[...], 1, 1).astype(own.dtype)
        far[...] = dot(put_far, grad[...], 1, 1).astype(far.dtype)


def bf16(*shape):
    return jax.ShapeDtypeStruct(shape, jnp.bfloat16)


def table(x):
    return jax.ShapeDtypeStruct(x.shape, x.dtype)


def local(query_rows, key_rows, value_rows, grad_hosted, image_grid, destination):
    ranks = lax.axis_size("dp")
    slot = lax.axis_index("seq")
    image_grid = jnp.transpose(image_grid, (1, 2, 0))
    destination = jnp.transpose(destination)
    part_rows, width = query_rows.shape
    slot_rows = grad_hosted.shape[0]
    heads = width // HEAD_DIM
    block = slot_rows // ranks
    by_pairs = ranks == len(STEPS) and block % 16 == 0
    flops = 2 * slot_rows * slot_rows * width
    exps = slot_rows * slot_rows * heads

    def swap(x):
        return lax.ppermute(x, "seq", [(0, 1), (1, 0)])

    def call(kernel, ins, outs, params, name, scratch=(), work=0, out_spec=VMEM, sems=0):
        return pl.pallas_call(
            kernel,
            out_shape=outs,
            in_specs=[SMEM if x.dtype == jnp.int32 else VMEM for x in ins],
            out_specs=[out_spec] * len(outs),
            scratch_shapes=[pltpu.VMEM(shape, jnp.bfloat16) for shape in scratch]
            + [pltpu.SemaphoreType.DMA((sems,))] * (sems > 0),
            compiler_params=params,
            cost_estimate=pl.CostEstimate(
                flops=work * flops + 1,
                bytes_accessed=sum(x.size * x.dtype.itemsize for x in (*ins, *outs)),
                transcendentals=exps if work else 0,
            ),
            name=name,
        )(*ins)

    def spread(x):
        return lax.all_to_all(x, "dp", 0, 0, tiled=True)

    def exchange(blocks):
        return [
            lax.ppermute(x, "dp", [(rank, rank ^ step) for rank in range(ranks)]) if step else x
            for step, x in zip(STEPS, blocks)
        ]

    rows = []
    for x in (query_rows, key_rows, value_rows):
        rows += [x, swap(x)]
    grad_spread = spread(grad_hosted.reshape(ranks, block, width))
    k_img, v_img, q_turned, out_turned, lse, *attended = call(
        forward_kernel,
        (image_grid, *rows),
        [bf16(slot_rows, width)] * 2
        + [bf16(width, slot_rows)] * 2
        + [jax.ShapeDtypeStruct((heads, slot_rows), jnp.float32)]
        + ([bf16(block, width)] * ranks if by_pairs else [bf16(slot_rows, width)]),
        LARGE,
        "attend",
        scratch=[(slot_rows, width), (width, slot_rows), (slot_rows, width)],
        work=2,
    )
    if by_pairs:
        attended = exchange(attended)
        messages = call(
            to_lister_kernel,
            (destination, grad_spread),
            [bf16(block, width)] * ranks,
            SMALL,
            "to_lister",
        )
        host_order, grad_slot = call(
            to_host_kernel,
            (destination, *attended, *exchange(messages)),
            [bf16(ranks, block, width), bf16(slot_rows, width)],
            SMALL,
            "to_host",
        )
        (hosted_out,) = call(
            store_kernel,
            (spread(host_order),),
            [bf16(slot_rows, width)],
            SMALL,
            "store",
            out_spec=HBM,
            sems=ranks,
        )
    else:
        dest = lax.dynamic_index_in_dim(destination, slot, 0, keepdims=False)
        rank_ids = jnp.arange(ranks, dtype=jnp.int32)
        source = jnp.sum(
            jnp.where(dest[None, :] == rank_ids[:, None], rank_ids[None, :], 0), axis=1
        )
        both = spread(
            jnp.concatenate([grad_spread[dest], attended[0].reshape(ranks, block, width)], axis=1)
        )
        grad_slot = both[:, :block].reshape(slot_rows, width)
        hosted_out = spread(both[source, block:]).reshape(slot_rows, width)
    grads = call(
        backward_kernel,
        (image_grid, k_img, v_img, q_turned, out_turned, lse, grad_slot),
        [bf16(part_rows, width)] * 6,
        LARGE,
        "attend_back",
        scratch=[(width, slot_rows)] * 5,
        work=5,
    )
    grad_query, grad_key, grad_value = call(
        join_kernel,
        (*grads[:3], *(swap(x) for x in grads[3:])),
        [bf16(part_rows, width)] * 3,
        SMALL,
        "join",
        scratch=[(part_rows, width)] * 3,
        out_spec=HBM,
        sems=3,
    )
    return hosted_out, grad_query, grad_key, grad_value


def solution(mesh):
    rows = P(("groups", "dp", "seq"), None)
    return jax.shard_map(
        local,
        mesh=mesh,
        in_specs=(rows, rows, rows, rows, P("groups", None, None), P("groups", None)),
        out_specs=(rows,) * 4,
        check_vma=False,
    )
```

```python
import jax
import jax.numpy as jnp
from jax import lax
from jax.experimental import pallas as pl
from jax.experimental.pallas import tpu as pltpu
from jax.sharding import PartitionSpec as P


HEAD_DIM = 80
STRIP = 256
STEPS = (0, 7, 1, 2, 5, 3, 4, 6)
LAST = 2
LARGE = pltpu.CompilerParams(vmem_limit_bytes=12 * 1024 * 1024)
SMALL = pltpu.CompilerParams(vmem_limit_bytes=6 * 1024 * 1024)
SMEM = pl.BlockSpec(memory_space=pltpu.SMEM)
VMEM = pl.BlockSpec(memory_space=pltpu.VMEM)
HBM = pl.BlockSpec(memory_space=pltpu.HBM)


def dot(a, b, a_dim, b_dim):
    return lax.dot_general(
        a, b, (((a_dim,), (b_dim,)), ((), ())), preferred_element_type=jnp.float32
    )


def one_hot(condition):
    return jnp.where(condition, 1.0, 0.0).astype(jnp.bfloat16)


def iota(shape, dim):
    return lax.broadcasted_iota(jnp.int32, shape, dim)


def strips(width):
    return [slice(at, at + STRIP) for at in range(0, width, STRIP)]


def length_of(grid_ref, rank, image):
    return grid_ref[image, 0, rank] * grid_ref[image, 1, rank]


def image_place(grid_ref, rank, slot):
    start = jnp.int32(0)
    length = jnp.int32(0)
    for image in range(grid_ref.shape[0]):
        patches = length_of(grid_ref, rank, image)
        start = start + jnp.where(image < slot, patches, 0)
        length = jnp.where(image == slot, patches, length)
    return start, length


def row_pick(slot_rows, part_rows, first, start, length, transposed=False):
    shape = (part_rows, slot_rows) if transposed else (slot_rows, part_rows)
    offset = iota(shape, 1 if transposed else 0)
    row = iota(shape, 0 if transposed else 1) + first
    return one_hot((row == start + offset) & (offset < length))


def eye(n):
    return one_hot(iota((n, n), 0) == iota((n, n), 1))


def turn(identity, block):
    return dot(identity, block, 1, 1)


def block_of(to, rows):
    return pl.ds(pl.multiple_of(to * rows, rows), rows)


def to_lister_kernel(dest_ref, in_ref, *out_refs):
    rank = lax.axis_index("dp")
    slot = lax.axis_index("seq")
    for step, out_ref in zip(STEPS, out_refs):
        out_ref[...] = in_ref[dest_ref[slot, rank ^ step]]


def to_host_kernel(dest_ref, *refs):
    rank = lax.axis_index("dp")
    slot = lax.axis_index("seq")
    count = len(STEPS)
    o_refs, g_refs, (out_ref, grad_ref) = refs[:count], refs[count:-2], refs[-2:]
    rows = out_ref.shape[1]
    for step, o_ref in zip(STEPS, o_refs):
        out_ref[dest_ref[slot, rank ^ step]] = o_ref[...]
    for step, g_ref in zip(STEPS, g_refs):
        grad_ref[block_of(rank ^ step, rows), :] = g_ref[...]
    for step in STEPS[len(g_refs) :]:
        grad_ref[block_of(rank ^ step, rows), :] = jnp.zeros((rows, grad_ref.shape[1]), jnp.bfloat16)


def store_kernel(in_ref, hbm_ref, sems):
    rows = in_ref.shape[1]
    stores = [
        pltpu.make_async_copy(
            in_ref.at[index], hbm_ref.at[pl.ds(index * rows, rows)], sems.at[index]
        )
        for index in range(in_ref.shape[0])
    ]
    for store in stores:
        store.start()
    for store in stores:
        store.wait()


def join_kernel(*refs):
    hbm_refs, vmem_refs, sems = refs[6:9], refs[9:12], refs[12]
    stores = [
        pltpu.make_async_copy(vmem, hbm, sems.at[index])
        for index, (vmem, hbm) in enumerate(zip(vmem_refs, hbm_refs))
    ]
    for own, far, vmem, store in zip(refs[:3], refs[3:6], vmem_refs, stores):
        vmem[...] = own[...] + far[...]
        store.start()
    for store in stores:
        store.wait()


def forward_kernel(grid_ref, *refs):
    rows, (k_img, v_img, qt_ref, ot_ref, lse_ref), refs = refs[:6], refs[6:11], refs[11:]
    out_refs, (q_img, vt_ref, out_rows) = refs[:-3], refs[-3:]
    rank = lax.axis_index("dp")
    slot = lax.axis_index("seq")
    start, length = image_place(grid_ref, rank, slot)
    slot_rows, width = k_img.shape
    part_rows = rows[0].shape[0]
    inv_root = HEAD_DIM**-0.5
    pick_own = row_pick(slot_rows, part_rows, slot * part_rows, start, length)
    pick_far = row_pick(slot_rows, part_rows, (1 - slot) * part_rows, start, length)
    for own, far, image in zip(rows[0::2], rows[1::2], (q_img, k_img, v_img)):
        image[...] = (dot(pick_own, own[...], 1, 0) + dot(pick_far, far[...], 1, 0)).astype(
            image.dtype
        )
    identity = eye(slot_rows)
    for part in strips(width):
        qt_ref[part] = turn(identity, q_img[:, part]).astype(qt_ref.dtype)
        vt_ref[part] = turn(identity, v_img[:, part]).astype(vt_ref.dtype)
    key_bias = jnp.where(iota((slot_rows, 1), 0) < length, 0.0, -1e30)
    live = iota((1, slot_rows), 1) < length
    parts = [slice(at, at + HEAD_DIM) for at in range(0, width, HEAD_DIM)]
    raws = {}
    late = []

    def finish():
        part, probs = late.pop(0)
        ot_ref[part] = dot(vt_ref[part], probs, 1, 0).astype(ot_ref.dtype)

    for head, part in enumerate(parts):
        for other in range(head, min(head + 1 + 2, len(parts))):
            if other not in raws:
                raws[other] = dot(k_img[:, parts[other]], qt_ref[parts[other]], 1, 0)
        if len(late) > 1:
            finish()
        scores = raws[head] * inv_root + key_bias
        top = jnp.max(scores, axis=0, keepdims=True)
        weights = jnp.exp(scores - top)
        total = jnp.sum(weights, axis=0, keepdims=True)
        probs = (weights * jnp.where(live, 1.0 / total, 0.0)).astype(jnp.bfloat16)
        lse_ref[head : head + 1] = top + jnp.log(total)
        late.append((part, probs))
    while late:
        finish()
    for part in strips(width):
        out_rows[:, part] = turn(identity, ot_ref[part]).astype(out_rows.dtype)
    if len(out_refs) > 1:
        for step, out_ref in zip(STEPS, out_refs):
            out_ref[...] = out_rows[block_of(rank ^ step, out_ref.shape[0]), :]
    else:
        out_refs[0][...] = out_rows[...]


def backward_kernel(grid_ref, *refs):
    (k_img, v_img, qt_ref, ot_ref, lse_ref), refs = refs[:5], refs[5:]
    (g_ref, *last_refs), refs = refs[:-12], refs[-12:]
    own_refs, far_refs, (g_img, gt_ref, kt_ref, *grad_refs) = refs[:3], refs[3:6], refs[6:]
    g_img[...] = g_ref[...]
    for step, last_ref in zip(STEPS[-LAST:], last_refs):
        to = lax.axis_index("dp") ^ step
        g_img[block_of(to, last_ref.shape[0]), :] = last_ref[...]
    rank = lax.axis_index("dp")
    slot = lax.axis_index("seq")
    start, length = image_place(grid_ref, rank, slot)
    slot_rows, width = k_img.shape
    part_rows = own_refs[0].shape[0]
    inv_root = HEAD_DIM**-0.5
    identity = eye(slot_rows)
    live = iota((1, slot_rows), 1) < length
    for part in strips(width):
        gt_ref[part] = jnp.where(live, turn(identity, g_img[:, part]), 0.0).astype(gt_ref.dtype)
        kt_ref[part] = turn(identity, k_img[:, part]).astype(kt_ref.dtype)
    key_bias = jnp.where(iota((slot_rows, 1), 0) < length, 0.0, -1e30)
    dq_ref, dk_ref, dv_ref = grad_refs
    parts = [slice(at, at + HEAD_DIM) for at in range(0, width, HEAD_DIM)]
    raws = {}
    late = []

    def finish():
        part, probs, grad_scores = late.pop(0)
        dq_ref[part] = dot(kt_ref[part], grad_scores, 1, 0).astype(dq_ref.dtype)
        dk_ref[part] = dot(qt_ref[part], grad_scores, 1, 1).astype(dk_ref.dtype)
        dv_ref[part] = dot(gt_ref[part], probs, 1, 1).astype(dv_ref.dtype)

    for head, part in enumerate(parts):
        for other in range(head, min(head + 1 + 1, len(parts))):
            if other not in raws:
                at = parts[other]
                raws[other] = (dot(k_img[:, at], qt_ref[at], 1, 0), dot(v_img[:, at], gt_ref[at], 1, 0))
        if len(late) > 0:
            finish()
        raw, grad_probs = raws.pop(head)
        raws[head] = None
        probs = jnp.exp(raw * inv_root + key_bias - lse_ref[head : head + 1])
        row_dot = jnp.sum(
            gt_ref[part].astype(jnp.float32) * ot_ref[part].astype(jnp.float32), axis=0, keepdims=True
        )
        grad_scores = (probs * (grad_probs - row_dot) * inv_root).astype(jnp.bfloat16)
        late.append((part, probs.astype(jnp.bfloat16), grad_scores))
    while late:
        finish()
    put_own = row_pick(slot_rows, part_rows, slot * part_rows, start, length, True)
    put_far = row_pick(slot_rows, part_rows, (1 - slot) * part_rows, start, length, True)
    for grad, own, far in zip(grad_refs, own_refs, far_refs):
        own[...] = dot(put_own, grad[...], 1, 1).astype(own.dtype)
        far[...] = dot(put_far, grad[...], 1, 1).astype(far.dtype)


def bf16(*shape):
    return jax.ShapeDtypeStruct(shape, jnp.bfloat16)


def table(x):
    return jax.ShapeDtypeStruct(x.shape, x.dtype)


def local(query_rows, key_rows, value_rows, grad_hosted, image_grid, destination):
    ranks = lax.axis_size("dp")
    slot = lax.axis_index("seq")
    image_grid = jnp.transpose(image_grid, (1, 2, 0))
    destination = jnp.transpose(destination)
    part_rows, width = query_rows.shape
    slot_rows = grad_hosted.shape[0]
    heads = width // HEAD_DIM
    block = slot_rows // ranks
    by_pairs = ranks == len(STEPS) and block % 16 == 0
    flops = 2 * slot_rows * slot_rows * width
    exps = slot_rows * slot_rows * heads

    def swap(x):
        return lax.ppermute(x, "seq", [(0, 1), (1, 0)])

    def call(kernel, ins, outs, params, name, scratch=(), work=0, out_spec=VMEM, sems=0):
        return pl.pallas_call(
            kernel,
            out_shape=outs,
            in_specs=[SMEM if x.dtype == jnp.int32 else VMEM for x in ins],
            out_specs=[out_spec] * len(outs),
            scratch_shapes=[pltpu.VMEM(shape, jnp.bfloat16) for shape in scratch]
            + [pltpu.SemaphoreType.DMA((sems,))] * (sems > 0),
            compiler_params=params,
            cost_estimate=pl.CostEstimate(
                flops=work * flops + 1,
                bytes_accessed=sum(x.size * x.dtype.itemsize for x in (*ins, *outs)),
                transcendentals=exps if work else 0,
            ),
            name=name,
        )(*ins)

    def spread(x):
        return lax.all_to_all(x, "dp", 0, 0, tiled=True)

    def exchange(blocks):
        return [
            lax.ppermute(x, "dp", [(rank, rank ^ step) for rank in range(ranks)]) if step else x
            for step, x in zip(STEPS, blocks)
        ]

    rows = []
    for x in (query_rows, key_rows, value_rows):
        rows += [x, swap(x)]
    grad_spread = spread(grad_hosted.reshape(ranks, block, width))
    k_img, v_img, q_turned, out_turned, lse, *attended = call(
        forward_kernel,
        (image_grid, *rows),
        [bf16(slot_rows, width)] * 2
        + [bf16(width, slot_rows)] * 2
        + [jax.ShapeDtypeStruct((heads, slot_rows), jnp.float32)]
        + ([bf16(block, width)] * ranks if by_pairs else [bf16(slot_rows, width)]),
        LARGE,
        "attend",
        scratch=[(slot_rows, width), (width, slot_rows), (slot_rows, width)],
        work=2,
    )
    if by_pairs:
        attended = exchange(attended)
        messages = call(
            to_lister_kernel,
            (destination, grad_spread),
            [bf16(block, width)] * ranks,
            SMALL,
            "to_lister",
        )
        grad_blocks = exchange(messages)
        host_order, grad_slot = call(
            to_host_kernel,
            (destination, *attended, *grad_blocks[:-LAST]),
            [bf16(ranks, block, width), bf16(slot_rows, width)],
            SMALL,
            "to_host",
        )
        host_order, *last = lax.optimization_barrier((host_order, *grad_blocks[-LAST:]))
        (hosted_out,) = call(
            store_kernel,
            (spread(host_order),),
            [bf16(slot_rows, width)],
            SMALL,
            "store",
            out_spec=HBM,
            sems=ranks,
        )
    else:
        dest = lax.dynamic_index_in_dim(destination, slot, 0, keepdims=False)
        rank_ids = jnp.arange(ranks, dtype=jnp.int32)
        source = jnp.sum(
            jnp.where(dest[None, :] == rank_ids[:, None], rank_ids[None, :], 0), axis=1
        )
        both = spread(
            jnp.concatenate([grad_spread[dest], attended[0].reshape(ranks, block, width)], axis=1)
        )
        grad_slot, last = both[:, :block].reshape(slot_rows, width), []
        hosted_out = spread(both[source, block:]).reshape(slot_rows, width)
    grads = call(
        backward_kernel,
        (image_grid, k_img, v_img, q_turned, out_turned, lse, grad_slot, *last),
        [bf16(part_rows, width)] * 6,
        LARGE,
        "attend_back",
        scratch=[(slot_rows, width)] + [(width, slot_rows)] * 5,
        work=5,
    )
    grad_query, grad_key, grad_value = call(
        join_kernel,
        (*grads[:3], *(swap(x) for x in grads[3:])),
        [bf16(part_rows, width)] * 3,
        SMALL,
        "join",
        scratch=[(part_rows, width)] * 3,
        out_spec=HBM,
        sems=3,
    )
    return hosted_out, grad_query, grad_key, grad_value


def solution(mesh):
    rows = P(("groups", "dp", "seq"), None)
    return jax.shard_map(
        local,
        mesh=mesh,
        in_specs=(rows, rows, rows, rows, P("groups", None, None), P("groups", None)),
        out_specs=(rows,) * 4,
        check_vma=False,
    )
```

```python
import jax
import jax.numpy as jnp
from jax import lax
from jax.experimental import pallas as pl
from jax.experimental.pallas import tpu as pltpu
from jax.sharding import PartitionSpec as P


HEAD_DIM = 80
STRIP = 256
STEPS = (0, 6, 2, 5, 1, 3, 4, 7)
LAST = 2
LARGE = pltpu.CompilerParams(vmem_limit_bytes=12 * 1024 * 1024)
SMALL = pltpu.CompilerParams(vmem_limit_bytes=6 * 1024 * 1024)
SMEM = pl.BlockSpec(memory_space=pltpu.SMEM)
VMEM = pl.BlockSpec(memory_space=pltpu.VMEM)
HBM = pl.BlockSpec(memory_space=pltpu.HBM)


def dot(a, b, a_dim, b_dim):
    return lax.dot_general(
        a, b, (((a_dim,), (b_dim,)), ((), ())), preferred_element_type=jnp.float32
    )


def one_hot(condition):
    return jnp.where(condition, 1.0, 0.0).astype(jnp.bfloat16)


def iota(shape, dim):
    return lax.broadcasted_iota(jnp.int32, shape, dim)


def strips(width):
    return [slice(at, at + STRIP) for at in range(0, width, STRIP)]


def length_of(grid_ref, rank, image):
    return grid_ref[image, 0, rank] * grid_ref[image, 1, rank]


def image_place(grid_ref, rank, slot):
    start = jnp.int32(0)
    length = jnp.int32(0)
    for image in range(grid_ref.shape[0]):
        patches = length_of(grid_ref, rank, image)
        start = start + jnp.where(image < slot, patches, 0)
        length = jnp.where(image == slot, patches, length)
    return start, length


def row_pick(slot_rows, part_rows, first, start, length, transposed=False):
    shape = (part_rows, slot_rows) if transposed else (slot_rows, part_rows)
    offset = iota(shape, 1 if transposed else 0)
    row = iota(shape, 0 if transposed else 1) + first
    return one_hot((row == start + offset) & (offset < length))


def eye(n):
    return one_hot(iota((n, n), 0) == iota((n, n), 1))


def turn(identity, block):
    return dot(identity, block, 1, 1)


def block_of(to, rows):
    return pl.ds(pl.multiple_of(to * rows, rows), rows)


def to_lister_kernel(dest_ref, in_ref, *out_refs):
    rank = lax.axis_index("dp")
    slot = lax.axis_index("seq")
    for step, out_ref in zip(STEPS, out_refs):
        out_ref[...] = in_ref[dest_ref[slot, rank ^ step]]


def to_host_kernel(dest_ref, *refs):
    rank = lax.axis_index("dp")
    slot = lax.axis_index("seq")
    count = len(STEPS)
    o_refs, g_refs, (out_ref, grad_ref) = refs[:count], refs[count:-2], refs[-2:]
    rows = out_ref.shape[1]
    for step, o_ref in zip(STEPS, o_refs):
        out_ref[dest_ref[slot, rank ^ step]] = o_ref[...]
    for step, g_ref in zip(STEPS, g_refs):
        grad_ref[block_of(rank ^ step, rows), :] = g_ref[...]
    for step in STEPS[len(g_refs) :]:
        grad_ref[block_of(rank ^ step, rows), :] = jnp.zeros((rows, grad_ref.shape[1]), jnp.bfloat16)


def store_kernel(in_ref, hbm_ref, sems):
    rows = in_ref.shape[1]
    stores = [
        pltpu.make_async_copy(
            in_ref.at[index], hbm_ref.at[pl.ds(index * rows, rows)], sems.at[index]
        )
        for index in range(in_ref.shape[0])
    ]
    for store in stores:
        store.start()
    for store in stores:
        store.wait()


def join_kernel(*refs):
    hbm_refs, vmem_refs, sems = refs[6:9], refs[9:12], refs[12]
    stores = [
        pltpu.make_async_copy(vmem, hbm, sems.at[index])
        for index, (vmem, hbm) in enumerate(zip(vmem_refs, hbm_refs))
    ]
    for own, far, vmem, store in zip(refs[:3], refs[3:6], vmem_refs, stores):
        vmem[...] = own[...] + far[...]
        store.start()
    for store in stores:
        store.wait()


def forward_kernel(grid_ref, *refs):
    rows, (k_img, v_img, qt_ref, ot_ref, lse_ref), refs = refs[:6], refs[6:11], refs[11:]
    out_refs, (q_img, vt_ref, out_rows) = refs[:-3], refs[-3:]
    rank = lax.axis_index("dp")
    slot = lax.axis_index("seq")
    start, length = image_place(grid_ref, rank, slot)
    slot_rows, width = k_img.shape
    part_rows = rows[0].shape[0]
    inv_root = HEAD_DIM**-0.5
    pick_own = row_pick(slot_rows, part_rows, slot * part_rows, start, length)
    pick_far = row_pick(slot_rows, part_rows, (1 - slot) * part_rows, start, length)
    for own, far, image in zip(rows[0::2], rows[1::2], (q_img, k_img, v_img)):
        image[...] = (dot(pick_own, own[...], 1, 0) + dot(pick_far, far[...], 1, 0)).astype(
            image.dtype
        )
    identity = eye(slot_rows)
    for part in strips(width):
        qt_ref[part] = turn(identity, q_img[:, part]).astype(qt_ref.dtype)
        vt_ref[part] = turn(identity, v_img[:, part]).astype(vt_ref.dtype)
    key_bias = jnp.where(iota((slot_rows, 1), 0) < length, 0.0, -1e30)
    live = iota((1, slot_rows), 1) < length
    parts = [slice(at, at + HEAD_DIM) for at in range(0, width, HEAD_DIM)]
    raws = {}
    late = []

    def finish():
        part, probs = late.pop(0)
        ot_ref[part] = dot(vt_ref[part], probs, 1, 0).astype(ot_ref.dtype)

    for head, part in enumerate(parts):
        for other in range(head, min(head + 1 + 2, len(parts))):
            if other not in raws:
                raws[other] = dot(k_img[:, parts[other]], qt_ref[parts[other]], 1, 0)
        if len(late) > 1:
            finish()
        scores = raws[head] * inv_root + key_bias
        top = jnp.max(scores, axis=0, keepdims=True)
        weights = jnp.exp(scores - top)
        total = jnp.sum(weights, axis=0, keepdims=True)
        probs = (weights * jnp.where(live, 1.0 / total, 0.0)).astype(jnp.bfloat16)
        lse_ref[head : head + 1] = top + jnp.log(total)
        late.append((part, probs))
    while late:
        finish()
    for part in strips(width):
        out_rows[:, part] = turn(identity, ot_ref[part]).astype(out_rows.dtype)
    if len(out_refs) > 1:
        for step, out_ref in zip(STEPS, out_refs):
            out_ref[...] = out_rows[block_of(rank ^ step, out_ref.shape[0]), :]
    else:
        out_refs[0][...] = out_rows[...]


def backward_kernel(grid_ref, *refs):
    (k_img, v_img, qt_ref, ot_ref, lse_ref), refs = refs[:5], refs[5:]
    (g_ref, *last_refs), refs = refs[:-12], refs[-12:]
    own_refs, far_refs, (g_img, gt_ref, kt_ref, *grad_refs) = refs[:3], refs[3:6], refs[6:]
    g_img[...] = g_ref[...]
    for step, last_ref in zip(STEPS[-LAST:], last_refs):
        to = lax.axis_index("dp") ^ step
        g_img[block_of(to, last_ref.shape[0]), :] = last_ref[...]
    rank = lax.axis_index("dp")
    slot = lax.axis_index("seq")
    start, length = image_place(grid_ref, rank, slot)
    slot_rows, width = k_img.shape
    part_rows = own_refs[0].shape[0]
    inv_root = HEAD_DIM**-0.5
    identity = eye(slot_rows)
    live = iota((1, slot_rows), 1) < length
    for part in strips(width):
        gt_ref[part] = jnp.where(live, turn(identity, g_img[:, part]), 0.0).astype(gt_ref.dtype)
        kt_ref[part] = turn(identity, k_img[:, part]).astype(kt_ref.dtype)
    key_bias = jnp.where(iota((slot_rows, 1), 0) < length, 0.0, -1e30)
    dq_ref, dk_ref, dv_ref = grad_refs
    parts = [slice(at, at + HEAD_DIM) for at in range(0, width, HEAD_DIM)]
    raws = {}
    late = []

    def finish():
        part, probs, grad_scores = late.pop(0)
        dq_ref[part] = dot(kt_ref[part], grad_scores, 1, 0).astype(dq_ref.dtype)
        dk_ref[part] = dot(qt_ref[part], grad_scores, 1, 1).astype(dk_ref.dtype)
        dv_ref[part] = dot(gt_ref[part], probs, 1, 1).astype(dv_ref.dtype)

    for head, part in enumerate(parts):
        for other in range(head, min(head + 1 + 1, len(parts))):
            if other not in raws:
                at = parts[other]
                raws[other] = (dot(k_img[:, at], qt_ref[at], 1, 0), dot(v_img[:, at], gt_ref[at], 1, 0))
        if len(late) > 0:
            finish()
        raw, grad_probs = raws.pop(head)
        raws[head] = None
        probs = jnp.exp(raw * inv_root + key_bias - lse_ref[head : head + 1])
        row_dot = jnp.sum(
            gt_ref[part].astype(jnp.float32) * ot_ref[part].astype(jnp.float32), axis=0, keepdims=True
        )
        grad_scores = (probs * (grad_probs - row_dot) * inv_root).astype(jnp.bfloat16)
        late.append((part, probs.astype(jnp.bfloat16), grad_scores))
    while late:
        finish()
    put_own = row_pick(slot_rows, part_rows, slot * part_rows, start, length, True)
    put_far = row_pick(slot_rows, part_rows, (1 - slot) * part_rows, start, length, True)
    for grad, own, far in zip(grad_refs, own_refs, far_refs):
        own[...] = dot(put_own, grad[...], 1, 1).astype(own.dtype)
        far[...] = dot(put_far, grad[...], 1, 1).astype(far.dtype)


def bf16(*shape):
    return jax.ShapeDtypeStruct(shape, jnp.bfloat16)


def table(x):
    return jax.ShapeDtypeStruct(x.shape, x.dtype)


def local(query_rows, key_rows, value_rows, grad_hosted, image_grid, destination):
    ranks = lax.axis_size("dp")
    slot = lax.axis_index("seq")
    image_grid = jnp.transpose(image_grid, (1, 2, 0))
    destination = jnp.transpose(destination)
    part_rows, width = query_rows.shape
    slot_rows = grad_hosted.shape[0]
    heads = width // HEAD_DIM
    block = slot_rows // ranks
    by_pairs = ranks == len(STEPS) and block % 16 == 0
    flops = 2 * slot_rows * slot_rows * width
    exps = slot_rows * slot_rows * heads

    def swap(x):
        return lax.ppermute(x, "seq", [(0, 1), (1, 0)])

    def call(kernel, ins, outs, params, name, scratch=(), work=0, out_spec=VMEM, sems=0):
        return pl.pallas_call(
            kernel,
            out_shape=outs,
            in_specs=[SMEM if x.dtype == jnp.int32 else VMEM for x in ins],
            out_specs=[out_spec] * len(outs),
            scratch_shapes=[pltpu.VMEM(shape, jnp.bfloat16) for shape in scratch]
            + [pltpu.SemaphoreType.DMA((sems,))] * (sems > 0),
            compiler_params=params,
            cost_estimate=pl.CostEstimate(
                flops=work * flops + 1,
                bytes_accessed=sum(x.size * x.dtype.itemsize for x in (*ins, *outs)),
                transcendentals=exps if work else 0,
            ),
            name=name,
        )(*ins)

    def spread(x):
        return lax.all_to_all(x, "dp", 0, 0, tiled=True)

    def exchange(blocks):
        return [
            lax.ppermute(x, "dp", [(rank, rank ^ step) for rank in range(ranks)]) if step else x
            for step, x in zip(STEPS, blocks)
        ]

    rows = []
    for x in (query_rows, key_rows, value_rows):
        rows += [x, swap(x)]
    grad_spread = spread(grad_hosted.reshape(ranks, block, width))
    k_img, v_img, q_turned, out_turned, lse, *attended = call(
        forward_kernel,
        (image_grid, *rows),
        [bf16(slot_rows, width)] * 2
        + [bf16(width, slot_rows)] * 2
        + [jax.ShapeDtypeStruct((heads, slot_rows), jnp.float32)]
        + ([bf16(block, width)] * ranks if by_pairs else [bf16(slot_rows, width)]),
        LARGE,
        "attend",
        scratch=[(slot_rows, width), (width, slot_rows), (slot_rows, width)],
        work=2,
    )
    if by_pairs:
        attended = exchange(attended)
        messages = call(
            to_lister_kernel,
            (destination, grad_spread),
            [bf16(block, width)] * ranks,
            SMALL,
            "to_lister",
        )
        grad_blocks = exchange(messages)
        host_order, grad_slot = call(
            to_host_kernel,
            (destination, *attended, *grad_blocks[:-LAST]),
            [bf16(ranks, block, width), bf16(slot_rows, width)],
            SMALL,
            "to_host",
        )
        host_order, *last = lax.optimization_barrier((host_order, *grad_blocks[-LAST:]))
        (hosted_out,) = call(
            store_kernel,
            (spread(host_order),),
            [bf16(slot_rows, width)],
            SMALL,
            "store",
            out_spec=HBM,
            sems=ranks,
        )
    else:
        dest = lax.dynamic_index_in_dim(destination, slot, 0, keepdims=False)
        rank_ids = jnp.arange(ranks, dtype=jnp.int32)
        source = jnp.sum(
            jnp.where(dest[None, :] == rank_ids[:, None], rank_ids[None, :], 0), axis=1
        )
        both = spread(
            jnp.concatenate([grad_spread[dest], attended[0].reshape(ranks, block, width)], axis=1)
        )
        grad_slot, last = both[:, :block].reshape(slot_rows, width), []
        hosted_out = spread(both[source, block:]).reshape(slot_rows, width)
    grads = call(
        backward_kernel,
        (image_grid, k_img, v_img, q_turned, out_turned, lse, grad_slot, *last),
        [bf16(part_rows, width)] * 6,
        LARGE,
        "attend_back",
        scratch=[(slot_rows, width)] + [(width, slot_rows)] * 5,
        work=5,
    )
    grad_query, grad_key, grad_value = call(
        join_kernel,
        (*grads[:3], *(swap(x) for x in grads[3:])),
        [bf16(part_rows, width)] * 3,
        SMALL,
        "join",
        scratch=[(part_rows, width)] * 3,
        out_spec=HBM,
        sems=3,
    )
    return hosted_out, grad_query, grad_key, grad_value


def solution(mesh):
    rows = P(("groups", "dp", "seq"), None)
    return jax.shard_map(
        local,
        mesh=mesh,
        in_specs=(rows, rows, rows, rows, P("groups", None, None), P("groups", None)),
        out_specs=(rows,) * 4,
        check_vma=False,
    )
```

```python
import jax
import jax.numpy as jnp
from jax import lax
from jax.experimental import pallas as pl
from jax.experimental.pallas import tpu as pltpu
from jax.sharding import PartitionSpec as P


HEAD_DIM = 80
STRIP = 256
STEPS = (0, 6, 2, 5, 1, 3, 4, 7)
LAST = 2
HELD = 2
LARGE = pltpu.CompilerParams(vmem_limit_bytes=12 * 1024 * 1024)
SMALL = pltpu.CompilerParams(vmem_limit_bytes=6 * 1024 * 1024)
SMEM = pl.BlockSpec(memory_space=pltpu.SMEM)
VMEM = pl.BlockSpec(memory_space=pltpu.VMEM)
HBM = pl.BlockSpec(memory_space=pltpu.HBM)


def dot(a, b, a_dim, b_dim):
    return lax.dot_general(
        a, b, (((a_dim,), (b_dim,)), ((), ())), preferred_element_type=jnp.float32
    )


def one_hot(condition):
    return jnp.where(condition, 1.0, 0.0).astype(jnp.bfloat16)


def iota(shape, dim):
    return lax.broadcasted_iota(jnp.int32, shape, dim)


def strips(width):
    return [slice(at, at + STRIP) for at in range(0, width, STRIP)]


def length_of(grid_ref, rank, image):
    return grid_ref[image, 0, rank] * grid_ref[image, 1, rank]


def image_place(grid_ref, rank, slot):
    start = jnp.int32(0)
    length = jnp.int32(0)
    for image in range(grid_ref.shape[0]):
        patches = length_of(grid_ref, rank, image)
        start = start + jnp.where(image < slot, patches, 0)
        length = jnp.where(image == slot, patches, length)
    return start, length


def row_pick(slot_rows, part_rows, first, start, length, transposed=False):
    shape = (part_rows, slot_rows) if transposed else (slot_rows, part_rows)
    offset = iota(shape, 1 if transposed else 0)
    row = iota(shape, 0 if transposed else 1) + first
    return one_hot((row == start + offset) & (offset < length))


def eye(n):
    return one_hot(iota((n, n), 0) == iota((n, n), 1))


def turn(identity, block):
    return dot(identity, block, 1, 1)


def block_of(to, rows):
    return pl.ds(pl.multiple_of(to * rows, rows), rows)


def to_lister_kernel(dest_ref, in_ref, *refs):
    rank = lax.axis_index("dp")
    slot = lax.axis_index("seq")
    o_refs, out_refs = refs[:HELD], refs[HELD:]
    for step, out_ref in zip(STEPS, out_refs):
        out_ref[...] = in_ref[dest_ref[slot, rank ^ step]]
    for o_ref, out_ref in zip(o_refs, out_refs[len(STEPS) :]):
        out_ref[...] = o_ref[...]


def to_host_kernel(dest_ref, *refs):
    rank = lax.axis_index("dp")
    slot = lax.axis_index("seq")
    count = len(STEPS)
    o_refs, g_refs, (out_ref, grad_ref) = refs[:count], refs[count:-2], refs[-2:]
    rows = out_ref.shape[1]
    for step, o_ref in zip(STEPS, o_refs):
        out_ref[dest_ref[slot, rank ^ step]] = o_ref[...]
    for step, g_ref in zip(STEPS, g_refs):
        grad_ref[block_of(rank ^ step, rows), :] = g_ref[...]
    for step in STEPS[len(g_refs) :]:
        grad_ref[block_of(rank ^ step, rows), :] = jnp.zeros((rows, grad_ref.shape[1]), jnp.bfloat16)


def store_kernel(in_ref, hbm_ref, sems):
    rows = in_ref.shape[1]
    stores = [
        pltpu.make_async_copy(
            in_ref.at[index], hbm_ref.at[pl.ds(index * rows, rows)], sems.at[index]
        )
        for index in range(in_ref.shape[0])
    ]
    for store in stores:
        store.start()
    for store in stores:
        store.wait()


def join_kernel(*refs):
    hbm_refs, vmem_refs, sems = refs[6:9], refs[9:12], refs[12]
    stores = [
        pltpu.make_async_copy(vmem, hbm, sems.at[index])
        for index, (vmem, hbm) in enumerate(zip(vmem_refs, hbm_refs))
    ]
    for own, far, vmem, store in zip(refs[:3], refs[3:6], vmem_refs, stores):
        vmem[...] = own[...] + far[...]
        store.start()
    for store in stores:
        store.wait()


def forward_kernel(grid_ref, *refs):
    rows, (k_img, v_img, qt_ref, ot_ref, lse_ref), refs = refs[:6], refs[6:11], refs[11:]
    out_refs, (q_img, vt_ref, out_rows) = refs[:-3], refs[-3:]
    rank = lax.axis_index("dp")
    slot = lax.axis_index("seq")
    start, length = image_place(grid_ref, rank, slot)
    slot_rows, width = k_img.shape
    part_rows = rows[0].shape[0]
    inv_root = HEAD_DIM**-0.5
    pick_own = row_pick(slot_rows, part_rows, slot * part_rows, start, length)
    pick_far = row_pick(slot_rows, part_rows, (1 - slot) * part_rows, start, length)
    for own, far, image in zip(rows[0::2], rows[1::2], (q_img, k_img, v_img)):
        image[...] = (dot(pick_own, own[...], 1, 0) + dot(pick_far, far[...], 1, 0)).astype(
            image.dtype
        )
    identity = eye(slot_rows)
    for part in strips(width):
        qt_ref[part] = turn(identity, q_img[:, part]).astype(qt_ref.dtype)
        vt_ref[part] = turn(identity, v_img[:, part]).astype(vt_ref.dtype)
    key_bias = jnp.where(iota((slot_rows, 1), 0) < length, 0.0, -1e30)
    live = iota((1, slot_rows), 1) < length
    parts = [slice(at, at + HEAD_DIM) for at in range(0, width, HEAD_DIM)]
    raws = {}
    late = []

    def finish():
        part, probs = late.pop(0)
        ot_ref[part] = dot(vt_ref[part], probs, 1, 0).astype(ot_ref.dtype)

    for head, part in enumerate(parts):
        for other in range(head, min(head + 1 + 2, len(parts))):
            if other not in raws:
                raws[other] = dot(k_img[:, parts[other]], qt_ref[parts[other]], 1, 0)
        if len(late) > 1:
            finish()
        scores = raws[head] * inv_root + key_bias
        top = jnp.max(scores, axis=0, keepdims=True)
        weights = jnp.exp(scores - top)
        total = jnp.sum(weights, axis=0, keepdims=True)
        probs = (weights * jnp.where(live, 1.0 / total, 0.0)).astype(jnp.bfloat16)
        lse_ref[head : head + 1] = top + jnp.log(total)
        late.append((part, probs))
    while late:
        finish()
    for part in strips(width):
        out_rows[:, part] = turn(identity, ot_ref[part]).astype(out_rows.dtype)
    if len(out_refs) > 1:
        for step, out_ref in zip(STEPS, out_refs):
            out_ref[...] = out_rows[block_of(rank ^ step, out_ref.shape[0]), :]
    else:
        out_refs[0][...] = out_rows[...]


def backward_kernel(grid_ref, *refs):
    (k_img, v_img, qt_ref, ot_ref, lse_ref), refs = refs[:5], refs[5:]
    (g_ref, *last_refs), refs = refs[:-12], refs[-12:]
    own_refs, far_refs, (g_img, gt_ref, kt_ref, *grad_refs) = refs[:3], refs[3:6], refs[6:]
    g_img[...] = g_ref[...]
    for step, last_ref in zip(STEPS[-LAST:], last_refs):
        to = lax.axis_index("dp") ^ step
        g_img[block_of(to, last_ref.shape[0]), :] = last_ref[...]
    rank = lax.axis_index("dp")
    slot = lax.axis_index("seq")
    start, length = image_place(grid_ref, rank, slot)
    slot_rows, width = k_img.shape
    part_rows = own_refs[0].shape[0]
    inv_root = HEAD_DIM**-0.5
    identity = eye(slot_rows)
    live = iota((1, slot_rows), 1) < length
    for part in strips(width):
        gt_ref[part] = jnp.where(live, turn(identity, g_img[:, part]), 0.0).astype(gt_ref.dtype)
        kt_ref[part] = turn(identity, k_img[:, part]).astype(kt_ref.dtype)
    key_bias = jnp.where(iota((slot_rows, 1), 0) < length, 0.0, -1e30)
    dq_ref, dk_ref, dv_ref = grad_refs
    parts = [slice(at, at + HEAD_DIM) for at in range(0, width, HEAD_DIM)]
    raws = {}
    late = []

    def finish():
        part, probs, grad_scores = late.pop(0)
        dq_ref[part] = dot(kt_ref[part], grad_scores, 1, 0).astype(dq_ref.dtype)
        dk_ref[part] = dot(qt_ref[part], grad_scores, 1, 1).astype(dk_ref.dtype)
        dv_ref[part] = dot(gt_ref[part], probs, 1, 1).astype(dv_ref.dtype)

    for head, part in enumerate(parts):
        for other in range(head, min(head + 1 + 1, len(parts))):
            if other not in raws:
                at = parts[other]
                raws[other] = (dot(k_img[:, at], qt_ref[at], 1, 0), dot(v_img[:, at], gt_ref[at], 1, 0))
        if len(late) > 0:
            finish()
        raw, grad_probs = raws.pop(head)
        raws[head] = None
        probs = jnp.exp(raw * inv_root + key_bias - lse_ref[head : head + 1])
        row_dot = jnp.sum(
            gt_ref[part].astype(jnp.float32) * ot_ref[part].astype(jnp.float32), axis=0, keepdims=True
        )
        grad_scores = (probs * (grad_probs - row_dot) * inv_root).astype(jnp.bfloat16)
        late.append((part, probs.astype(jnp.bfloat16), grad_scores))
    while late:
        finish()
    put_own = row_pick(slot_rows, part_rows, slot * part_rows, start, length, True)
    put_far = row_pick(slot_rows, part_rows, (1 - slot) * part_rows, start, length, True)
    for grad, own, far in zip(grad_refs, own_refs, far_refs):
        own[...] = dot(put_own, grad[...], 1, 1).astype(own.dtype)
        far[...] = dot(put_far, grad[...], 1, 1).astype(far.dtype)


def bf16(*shape):
    return jax.ShapeDtypeStruct(shape, jnp.bfloat16)


def table(x):
    return jax.ShapeDtypeStruct(x.shape, x.dtype)


def local(query_rows, key_rows, value_rows, grad_hosted, image_grid, destination):
    ranks = lax.axis_size("dp")
    slot = lax.axis_index("seq")
    image_grid = jnp.transpose(image_grid, (1, 2, 0))
    destination = jnp.transpose(destination)
    part_rows, width = query_rows.shape
    slot_rows = grad_hosted.shape[0]
    heads = width // HEAD_DIM
    block = slot_rows // ranks
    by_pairs = ranks == len(STEPS) and block % 16 == 0
    flops = 2 * slot_rows * slot_rows * width
    exps = slot_rows * slot_rows * heads

    def swap(x):
        return lax.ppermute(x, "seq", [(0, 1), (1, 0)])

    def call(kernel, ins, outs, params, name, scratch=(), work=0, out_spec=VMEM, sems=0):
        return pl.pallas_call(
            kernel,
            out_shape=outs,
            in_specs=[SMEM if x.dtype == jnp.int32 else VMEM for x in ins],
            out_specs=[out_spec] * len(outs),
            scratch_shapes=[pltpu.VMEM(shape, jnp.bfloat16) for shape in scratch]
            + [pltpu.SemaphoreType.DMA((sems,))] * (sems > 0),
            compiler_params=params,
            cost_estimate=pl.CostEstimate(
                flops=work * flops + 1,
                bytes_accessed=sum(x.size * x.dtype.itemsize for x in (*ins, *outs)),
                transcendentals=exps if work else 0,
            ),
            name=name,
        )(*ins)

    def spread(x):
        return lax.all_to_all(x, "dp", 0, 0, tiled=True)

    def exchange(blocks):
        return [
            lax.ppermute(x, "dp", [(rank, rank ^ step) for rank in range(ranks)]) if step else x
            for step, x in zip(STEPS, blocks)
        ]

    rows = []
    for x in (query_rows, key_rows, value_rows):
        rows += [x, swap(x)]
    grad_spread = spread(grad_hosted.reshape(ranks, block, width))
    k_img, v_img, q_turned, out_turned, lse, *attended = call(
        forward_kernel,
        (image_grid, *rows),
        [bf16(slot_rows, width)] * 2
        + [bf16(width, slot_rows)] * 2
        + [jax.ShapeDtypeStruct((heads, slot_rows), jnp.float32)]
        + ([bf16(block, width)] * ranks if by_pairs else [bf16(slot_rows, width)]),
        LARGE,
        "attend",
        scratch=[(slot_rows, width), (width, slot_rows), (slot_rows, width)],
        work=2,
    )
    if by_pairs:
        messages = call(
            to_lister_kernel,
            (destination, grad_spread, *attended[ranks - HELD :]),
            [bf16(block, width)] * (ranks + HELD),
            SMALL,
            "to_lister",
        )
        attended = exchange([*attended[: ranks - HELD], *messages[ranks:]])
        grad_blocks = exchange(messages[:ranks])
        host_order, grad_slot = call(
            to_host_kernel,
            (destination, *attended, *grad_blocks[:-LAST]),
            [bf16(ranks, block, width), bf16(slot_rows, width)],
            SMALL,
            "to_host",
        )
        host_order, *last = lax.optimization_barrier((host_order, *grad_blocks[-LAST:]))
        (hosted_out,) = call(
            store_kernel,
            (spread(host_order),),
            [bf16(slot_rows, width)],
            SMALL,
            "store",
            out_spec=HBM,
            sems=ranks,
        )
    else:
        dest = lax.dynamic_index_in_dim(destination, slot, 0, keepdims=False)
        rank_ids = jnp.arange(ranks, dtype=jnp.int32)
        source = jnp.sum(
            jnp.where(dest[None, :] == rank_ids[:, None], rank_ids[None, :], 0), axis=1
        )
        both = spread(
            jnp.concatenate([grad_spread[dest], attended[0].reshape(ranks, block, width)], axis=1)
        )
        grad_slot, last = both[:, :block].reshape(slot_rows, width), []
        hosted_out = spread(both[source, block:]).reshape(slot_rows, width)
    grads = call(
        backward_kernel,
        (image_grid, k_img, v_img, q_turned, out_turned, lse, grad_slot, *last),
        [bf16(part_rows, width)] * 6,
        LARGE,
        "attend_back",
        scratch=[(slot_rows, width)] + [(width, slot_rows)] * 5,
        work=5,
    )
    grad_query, grad_key, grad_value = call(
        join_kernel,
        (*grads[:3], *(swap(x) for x in grads[3:])),
        [bf16(part_rows, width)] * 3,
        SMALL,
        "join",
        scratch=[(part_rows, width)] * 3,
        out_spec=HBM,
        sems=3,
    )
    return hosted_out, grad_query, grad_key, grad_value


def solution(mesh):
    rows = P(("groups", "dp", "seq"), None)
    return jax.shard_map(
        local,
        mesh=mesh,
        in_specs=(rows, rows, rows, rows, P("groups", None, None), P("groups", None)),
        out_specs=(rows,) * 4,
        check_vma=False,
    )
```
